32 devices in a mesh: pw: 8 (over z, core), band: 4 (over y, x).
Axes of the slice: x: 2, y: 2, z: 4, core: 2. Of those that a mesh axis runs over, the one named last changes fastest.
Arguments:
- slab: bfloat16 [512, 2, 98304], P('band', None, 'pw'), may hold values from -0.01953125 to 0.01953125
- panel: float32 [16, 2, 98304], P('band', None, 'pw'), may hold values from -6 to 6
- potential: float32 [128, 128, 128], P('pw'), may hold values from -2 to 2
- pw_slot: int32 [98304], P('pw'), may hold values from 0 to 32767, as said below
- columns: int32 [2048], P('pw'), may hold values from 0 to 16383, as said below
Outputs:
- ritz_blocks: float32 [512, 64], P('band', 'pw')
The draws below stay inside these ranges and needn't reach their ends.
Inputs may be any that keep to these rules, and one draw needn't show every extreme that they name: Entry d * 256 + s is the grid column i1 * 128 + i2 of column slot s of index d of pw; all entries are distinct, and together they are the columns nearest the grid's third axis. `pw_slot`: the rows held by index d of pw are distinct values c * 128 + i3: the plane wave at third index i3 of column slot c of index d; within each device they are the cells of its columns nearest the grid's anchor.
All inputs are finite; a program needn't handle non-finite values.
Results may differ from the reference program's by a relative error of at most 0.0029.
Values may be sent and summed in bfloat16 or wider, within the bound.
A program may use at most 128 MiB of HBM per device.

```python
import jax
import jax.numpy as jnp
from jax import lax

N1 = 128
N2 = 128
N3 = 128
PW_DEV = 12288
COL_DEV = 256
NPW = 98304
BANDS = 512
PANEL = 16


def signed_index(index, length):
    return jnp.where(index < length // 2, index, index - length)


def sphere_map(key):
    blocks = NPW // PW_DEV
    total_cols = N1 * N2
    grid_cols = jnp.arange(total_cols, dtype=jnp.int32)
    first = signed_index(grid_cols // N2, N1)
    second = signed_index(grid_cols % N2, N2)
    ties = jax.random.permutation(jax.random.fold_in(key, 5), total_cols).astype(jnp.int32)
    ranks = (first * first + second * second) * total_cols + ties
    nearest = jnp.argsort(ranks, stable=True)[:COL_DEV * blocks].astype(jnp.int32)
    dealt = nearest.reshape(COL_DEV, blocks)[::-1].T
    slots = COL_DEV * N3
    slot_ids = jnp.arange(slots, dtype=jnp.int32)
    third = signed_index(slot_ids % N3, N3)

    def one_block(index):
        owned = dealt[index]
        holder = owned[slot_ids // N3]
        one = signed_index(holder // N2, N1)
        two = signed_index(holder % N2, N2)
        block_key = jax.random.fold_in(key, index + 100)
        block_ties = jax.random.permutation(jax.random.fold_in(block_key, 1), slots).astype(jnp.int32)
        block_ranks = (one * one + two * two + third * third) * slots + block_ties
        picked = jnp.argsort(block_ranks, stable=True)[:PW_DEV]
        shuffle = jax.random.permutation(jax.random.fold_in(block_key, 2), PW_DEV)
        return picked[shuffle].astype(jnp.int32)
    slot_rows = jax.vmap(one_block)(jnp.arange(blocks, dtype=jnp.int32)).reshape(-1)
    return (dealt.reshape(-1).astype(jnp.int32), slot_rows.astype(jnp.int32))


def draw_pw_slot(key, part):
    shared_cols, shared_slots = sphere_map(key)
    return shared_slots


def draw_columns(key, part):
    shared_cols, shared_slots = sphere_map(key)
    return shared_cols


def shard_levels(stream_key, extent, cuts, least, top_value):
    level = 1.0
    for position, parts in cuts:
        heights = jax.random.uniform(jax.random.fold_in(jax.random.fold_in(stream_key, 6), position), (parts,), jnp.float32, least / len(cuts), top_value / len(cuts))
        level = level * jnp.repeat(jnp.exp(heights), extent[position] // parts).reshape((-1,) + (1,) * (len(extent) - 1 - position))
    return level


def scatter_about(key, extent, width, most, pieces=(), held_as=jnp.bfloat16):
    drawn = jax.random.normal(key, extent, jnp.float32) * width
    if len(pieces) > 0:
        drawn = shard_levels(key, extent, pieces, -0.22, 0.18) * drawn
    return jnp.clip(drawn, min=-most, max=most).astype(held_as)


def setup_inputs(seed: int = 0) -> dict:
    arg_keys = jax.random.split(jax.random.key(seed), 6)
    return {
        "slab": scatter_about(arg_keys[0], (BANDS, 2, NPW), NPW ** -0.5, 0.01953125, ((0, 4), (2, 8))),
        "panel": scatter_about(arg_keys[1], (PANEL, 2, NPW), 1.0, 6.0, ((0, 4), (2, 8)), jnp.float32),
        "potential": jnp.clip(jax.random.uniform(arg_keys[2], (N3, N1, N2), jnp.float32, -2.0, 2.0) * shard_levels(arg_keys[2], (N3, N1, N2), ((0, 8),), -0.4, 0.0), -2.0, 2.0),
        "pw_slot": draw_pw_slot(jax.random.fold_in(arg_keys[5], 71), 0),
        "columns": draw_columns(jax.random.fold_in(arg_keys[5], 71), 0),
    }


def frequency(index, length):
    signed = jnp.where(index < length // 2, index, index - length)
    return signed.astype(jnp.float32) / (length / 2.0)


def kinetic_of(cells, first_len, second_len, third_len):
    first = cells // (second_len * third_len)
    second = (cells // third_len) % second_len
    third = cells % third_len
    fone = frequency(first, first_len)
    ftwo = frequency(second, second_len)
    fthree = frequency(third, third_len)
    return 0.5 * (fone * fone + ftwo * ftwo + fthree * fthree)


def make_kinds(pair):
    turned = jnp.stack([pair[:, 1], -pair[:, 0]], axis=1)
    return jnp.stack([pair, turned], axis=1)


def reference(slab, panel, potential, pw_slot, columns):
    owner = (jnp.arange(NPW, dtype=jnp.int32) // PW_DEV).astype(jnp.int32)
    column_index = (owner * COL_DEV + pw_slot // N3).astype(jnp.int32)
    pw_cell = (columns[column_index] * N3 + pw_slot % N3).astype(jnp.int32)
    kinetic = kinetic_of(pw_cell, N1, N2, N3)
    total = N1 * N2 * N3
    grid_potential = jnp.transpose(potential, (1, 2, 0))

    def apply_one(coeff_pair):
        real_part = jnp.zeros((total,), coeff_pair.dtype).at[pw_cell].set(coeff_pair[0])
        imag_part = jnp.zeros((total,), coeff_pair.dtype).at[pw_cell].set(coeff_pair[1])
        field = lax.complex(real_part, imag_part).reshape(N1, N2, N3)
        spread = jnp.fft.ifftn(field, norm="ortho")
        back = jnp.fft.fftn(grid_potential * spread, norm="ortho").reshape(-1)[pw_cell]
        return kinetic * coeff_pair + jnp.stack([jnp.real(back), jnp.imag(back)])

    applied = lax.map(apply_one, panel).astype(jnp.bfloat16)
    coeffs = panel.astype(jnp.bfloat16)
    operand = jnp.concatenate([make_kinds(applied), make_kinds(coeffs)], axis=1)
    operand = jnp.transpose(operand, (1, 0, 2, 3)).reshape(4 * PANEL, 2 * NPW)
    flat_slab = slab.reshape(BANDS, 2 * NPW)
    return jnp.dot(flat_slab, operand.T, preferred_element_type=jnp.float32)
```

```python
import functools
import math

import jax
import jax.numpy as jnp
import numpy as np
from jax import lax
from jax.experimental import pallas as pl
from jax.experimental.pallas import tpu as pltpu
from jax.sharding import PartitionSpec as P

F32 = jnp.float32
BF16 = jnp.bfloat16
NT = (((1,), (1,)), ((), ()))
TN = (((0,), (0,)), ((), ()))


def round_up(value, step):
    return -(-value // step) * step


def disk_square(first_len, second_len, count):
    one = np.arange(first_len) - first_len // 2
    two = np.arange(second_len) - second_len // 2
    return int(np.sort((one[:, None] ** 2 + two[None, :] ** 2).ravel())[count - 1])


def window(half, step, length):
    return min(round_up(2 * (half + 1), step), length)


def cos_sin(rows, cols, length):
    angles = 2.0 * np.pi / length * ((rows[:, None] * cols[None, :]) % length)
    factor = 1.0 / math.sqrt(length)
    return np.cos(angles) * factor, np.sin(angles) * factor


def signed_of(width):
    return np.arange(width) - width // 2


def z_tables(count, length, planes, width):
    devices = length // planes
    cos, sin = cos_sin(signed_of(width), np.arange(length), length)
    cos = cos.reshape(width, devices, planes)
    sin = sin.reshape(width, devices, planes)
    table = np.zeros((count, 2, width, devices, 2, count, planes), np.float32)
    for k in range(count):
        table[k, 0, :, :, 0, k] = cos
        table[k, 1, :, :, 0, k] = -sin
        table[k, 0, :, :, 1, k] = sin
        table[k, 1, :, :, 1, k] = cos
    size = count * 2
    return table.reshape(size * width, devices * size * planes)


def scatter_kernel(length, width, slot_ref, panel_ref, table_ref, out_ref, acc):
    step = pl.program_id(0)

    @pl.when(step == 0)
    def _():
        acc[...] = jnp.zeros_like(acc)

    slot = slot_ref[...]
    block = slot.shape[1]
    cols = acc.shape[1]
    col = slot // length
    third = lax.rem(lax.rem(slot, length) + width // 2, length)
    pick_col = (lax.broadcasted_iota(jnp.int32, (cols, block), 0) == col).astype(F32).astype(BF16)
    pick_third = (
        (lax.broadcasted_iota(jnp.int32, (width, block), 0) == third).astype(F32).astype(BF16)
    )
    values = panel_ref[...].astype(BF16)
    spread = jnp.concatenate(
        [pick_third * values[q : q + 1] for q in range(values.shape[0])], axis=0
    )
    acc[...] += lax.dot_general(spread, pick_col, NT, preferred_element_type=F32)

    @pl.when(step == pl.num_programs(0) - 1)
    def _():
        lanes = out_ref.shape[2]
        got = acc[...].astype(BF16)
        done = lax.dot_general(got, table_ref[...], TN, preferred_element_type=F32).astype(BF16)
        for d in range(out_ref.shape[0]):
            out_ref[d] = done[:, d * lanes : (d + 1) * lanes]


def scatter_z(slot, rows, table, cols, length, width, devices):
    count, n = rows.shape
    block = 1024
    lanes = table.shape[1] // devices
    return pl.pallas_call(
        functools.partial(scatter_kernel, length, width),
        grid=(n // block,),
        in_specs=[
            pl.BlockSpec((1, block), lambda i: (0, i)),
            pl.BlockSpec((count, block), lambda i: (0, i)),
            pl.BlockSpec(table.shape, lambda i: (0, 0)),
        ],
        out_specs=pl.BlockSpec((devices, cols, lanes), lambda i: (0, 0, 0)),
        out_shape=jax.ShapeDtypeStruct((devices, cols, lanes), BF16),
        scratch_shapes=[pltpu.VMEM((count * width, cols), F32)],
        compiler_params=pltpu.CompilerParams(vmem_limit_bytes=48 * 1024 * 1024),
        name="scatter_z",
    )(slot, rows, table)


def turn(tile, sign):
    half = tile.shape[1] // 2
    return jnp.concatenate([tile[:, half:], tile[:, :half]], axis=1) * sign


def plane_kernel(
    wide, n_one, n_two, pos_ref, x_ref, ty_ref, tx_ref, txb_ref, tyb_ref, v_ref, out_ref,
    wave, box, mid, vbuf, sem,
):
    total, lanes = wave.shape
    copy = pltpu.make_async_copy(v_ref, vbuf, sem)
    copy.start()
    sign = jnp.where(
        lax.broadcasted_iota(jnp.int32, (1, lanes), 1) < lanes // 2, -1.0, 1.0
    ).astype(F32)
    wave[...] = x_ref[...].astype(F32)
    box[...] = jnp.zeros_like(box)

    def put(step, carry):
        for u in range(16):
            c = step * 16 + u
            box[pl.ds(pos_ref[c], 1), :] = wave[pl.ds(c, 1), :]
        return carry

    lax.fori_loop(0, total // 16, put, 0)

    def stacked(tiles):
        plain = jnp.concatenate(tiles, axis=1)
        turned = jnp.concatenate([turn(tile, sign) for tile in tiles], axis=1)
        return jnp.concatenate([plain, turned], axis=0).astype(BF16)

    def inverse_two(step, carry):
        tiles = [box[pl.ds(pl.multiple_of((2 * step + u) * wide, 8), wide), :] for u in range(2)]
        got = jnp.dot(ty_ref[...], stacked(tiles), preferred_element_type=F32)
        for u in range(2):
            mid[pl.ds(2 * step + u, n_two, stride=wide), :] = got[:, u * lanes : (u + 1) * lanes]
        return carry

    lax.fori_loop(0, wide // 2, inverse_two, 0, unroll=2)
    copy.wait()

    def both_one(step, carry):
        starts = [pl.multiple_of((2 * step + u) * wide, 8) for u in range(2)]
        tiles = [mid[pl.ds(start, wide), :] for start in starts]
        got = jnp.dot(tx_ref[...], stacked(tiles), preferred_element_type=F32)
        got = got * vbuf[:, pl.ds(pl.multiple_of(step * 2 * lanes, 2 * lanes), 2 * lanes)]
        tiles = [got[:, u * lanes : (u + 1) * lanes] for u in range(2)]
        back = jnp.dot(txb_ref[...], stacked(tiles), preferred_element_type=F32)
        for u in range(2):
            mid[pl.ds(starts[u], wide), :] = back[:, u * lanes : (u + 1) * lanes]
        return carry

    lax.fori_loop(0, n_two // 2, both_one, 0, unroll=2)

    def forward_two(step, carry):
        tiles = [mid[pl.ds(2 * step + u, n_two, stride=wide), :] for u in range(2)]
        got = jnp.dot(tyb_ref[...], stacked(tiles), preferred_element_type=F32)
        for u in range(2):
            start = pl.multiple_of((2 * step + u) * wide, 8)
            box[pl.ds(start, wide), :] = got[:, u * lanes : (u + 1) * lanes]
        return carry

    lax.fori_loop(0, wide // 2, forward_two, 0, unroll=2)

    def take(step, carry):
        for u in range(16):
            c = step * 16 + u
            wave[pl.ds(c, 1), :] = box[pl.ds(pos_ref[c], 1), :]
        return carry

    lax.fori_loop(0, total // 16, take, 0)
    out_ref[...] = wave[...].astype(BF16)


def plane_part(pos, x, tables, potential_rows, wide, n_one, n_two):
    total, lanes = x.shape
    whole = pl.BlockSpec(memory_space=pltpu.VMEM)
    return pl.pallas_call(
        functools.partial(plane_kernel, wide, n_one, n_two),
        in_specs=[pl.BlockSpec(memory_space=pltpu.SMEM)]
        + [whole] * 5
        + [pl.BlockSpec(memory_space=pl.ANY)],
        out_specs=whole,
        out_shape=jax.ShapeDtypeStruct((total, lanes), BF16),
        scratch_shapes=[
            pltpu.VMEM((total, lanes), F32),
            pltpu.VMEM((wide * wide, lanes), F32),
            pltpu.VMEM((n_two * wide, lanes), F32),
            pltpu.VMEM(potential_rows.shape, F32),
            pltpu.SemaphoreType.DMA,
        ],
        compiler_params=pltpu.CompilerParams(vmem_limit_bytes=56 * 1024 * 1024),
        name="plane_part",
    )(pos, x, *tables, potential_rows)


def gather_kernel(
    lengths, width, slot_ref, panel_ref, x_ref, table_ref, marks_ref, out_ref, held
):
    n_one, n_two, length = lengths
    count = panel_ref.shape[0]
    body = count * width

    @pl.when(pl.program_id(0) == 0)
    def _():
        x = jnp.concatenate([x_ref[d] for d in range(x_ref.shape[0])], axis=1)
        held[:body, :] = lax.dot_general(
            table_ref[...], x, NT, preferred_element_type=F32
        ).astype(BF16)
        held[body:, :] = marks_ref[...]

    slot = slot_ref[...]
    block = slot.shape[1]
    cols = held.shape[1]
    col = slot // length
    third = lax.rem(slot, length)
    place = lax.rem(third + width // 2, length)
    pick_col = (lax.broadcasted_iota(jnp.int32, (cols, block), 0) == col).astype(F32).astype(BF16)
    at_third = lax.broadcasted_iota(jnp.int32, (width, block), 0) == place
    got = jnp.dot(held[...], pick_col, preferred_element_type=F32)
    f_one = got[body : body + 1] * (2.0 / n_one)
    f_two = got[body + 1 : body + 2] * (2.0 / n_two)
    f_three = jnp.where(third < length // 2, third, third - length).astype(F32) * (2.0 / length)
    kinetic = 0.5 * (f_one * f_one + f_two * f_two + f_three * f_three)
    picked = jnp.concatenate(
        [
            jnp.sum(
                jnp.where(at_third, got[q * width : (q + 1) * width], 0.0), axis=0, keepdims=True
            )
            for q in range(count)
        ],
        axis=0,
    )
    out_ref[...] = (kinetic * panel_ref[...] + picked).astype(BF16)


def gather_z(slot, rows, x, table, marks, lengths, width):
    count, n = rows.shape
    devices, cols, lanes = x.shape
    block = 1024
    return pl.pallas_call(
        functools.partial(gather_kernel, lengths, width),
        grid=(n // block,),
        in_specs=[
            pl.BlockSpec((1, block), lambda i: (0, i)),
            pl.BlockSpec((count, block), lambda i: (0, i)),
            pl.BlockSpec(x.shape, lambda i: (0, 0, 0)),
            pl.BlockSpec(table.shape, lambda i: (0, 0)),
            pl.BlockSpec(marks.shape, lambda i: (0, 0)),
        ],
        out_specs=pl.BlockSpec((count, block), lambda i: (0, i)),
        out_shape=jax.ShapeDtypeStruct((count, n), BF16),
        scratch_shapes=[pltpu.VMEM((count * width + marks.shape[0], cols), BF16)],
        compiler_params=pltpu.CompilerParams(vmem_limit_bytes=48 * 1024 * 1024),
        name="gather_z",
    )(slot, rows, x, table, marks)


def signed_index(index, length):
    return jnp.where(index < length // 2, index, index - length)


def per_device(slab, panel, potential, pw_slot, columns):
    devices = lax.axis_size("pw")
    planes, n_one, n_two = potential.shape
    length = planes * devices
    cols = columns.shape[0]
    count = panel.shape[0]
    n = panel.shape[2]
    lanes = 2 * count * planes

    square = disk_square(n_one, n_two, cols * devices)
    wide = window(math.isqrt(square), 64, max(n_one, n_two))
    reach = math.isqrt(square + (-(-n // (2 * cols)) + 2) ** 2) + 1
    width = window(reach, 16, length)

    ztab = z_tables(count, length, planes, width)
    cy, sy = cos_sin(np.arange(n_two), signed_of(wide), n_two)
    cx, sx = cos_sin(np.arange(n_one), signed_of(wide), n_one)
    tables = [
        np.concatenate([cy, sy], axis=1),
        np.concatenate([cx, sx], axis=1),
        np.concatenate([cx.T, -sx.T], axis=1),
        np.concatenate([cy.T, -sy.T], axis=1),
    ]
    tables = [jnp.asarray(t, BF16) for t in tables]
    ztab = jnp.asarray(ztab, BF16)

    coeffs = panel.astype(BF16)
    rows = panel.reshape(2 * count, n)
    slot = pw_slot.reshape(1, n)

    every_column = lax.all_gather(columns, "pw", axis=0, tiled=True)
    place_one = signed_index(every_column // n_two, n_one) + wide // 2
    place_two = signed_index(every_column % n_two, n_two) + wide // 2
    pos = place_one * wide + place_two
    mine = jnp.stack(
        [signed_index(columns // n_two, n_one), signed_index(columns % n_two, n_two)], axis=0
    )
    marks = jnp.concatenate([mine, jnp.zeros((14, cols), jnp.int32)], axis=0).astype(BF16)
    potential_rows = jnp.tile(
        jnp.transpose(potential, (1, 2, 0)), (1, 1, 2 * count)
    ).reshape(n_one, n_two * lanes)

    every_coeff = lax.all_gather(coeffs, "band", axis=0, tiled=True)
    sent = scatter_z(slot, rows, ztab, cols, length, width, devices)
    there = lax.all_to_all(sent, "pw", split_axis=0, concat_axis=0, tiled=True)
    worked = plane_part(
        pos, there.reshape(devices * cols, lanes), tables, potential_rows, wide, n_one, n_two
    )
    home = lax.all_to_all(
        worked.reshape(devices, cols, lanes), "pw", split_axis=0, concat_axis=0, tiled=True
    )
    applied = gather_z(slot, rows, home, ztab, marks, (n_one, n_two, length), width)
    every_applied = lax.all_gather(
        applied.reshape(count, 2, n), "band", axis=0, tiled=True
    )

    def project(piece):
        terms = jnp.einsum("jcw,nqw->cjqn", slab, piece, preferred_element_type=F32)
        return jnp.concatenate(
            [terms[0, :, 0] + terms[1, :, 1], terms[0, :, 1] - terms[1, :, 0]], axis=1
        )

    blocks = jnp.concatenate([project(every_applied), project(every_coeff)], axis=1)
    return lax.psum_scatter(blocks, "pw", scatter_dimension=1, tiled=True)


def solution(mesh):
    in_specs = (P("band", None, "pw"), P("band", None, "pw"), P("pw", None, None), P("pw"), P("pw"))
    out_specs = P("band", "pw")
    return jax.shard_map(
        per_device, mesh=mesh, in_specs=in_specs, out_specs=out_specs, check_vma=False
    )
```

```python
import functools
import math

import jax
import jax.numpy as jnp
import numpy as np
from jax import lax
from jax.experimental import pallas as pl
from jax.experimental.pallas import tpu as pltpu
from jax.sharding import PartitionSpec as P

F32 = jnp.float32
BF16 = jnp.bfloat16
NT = (((1,), (1,)), ((), ()))
TN = (((0,), (0,)), ((), ()))
MESH = pl.DeviceIdType.MESH
BLOCK = 1024
LIMIT = 56 * 1024 * 1024


def round_up(value, step):
    return -(-value // step) * step


def disk_square(first_len, second_len, count):
    one = np.arange(first_len) - first_len // 2
    two = np.arange(second_len) - second_len // 2
    return int(np.sort((one[:, None] ** 2 + two[None, :] ** 2).ravel())[count - 1])


def window(half, step, length):
    return min(round_up(2 * (half + 1), step), length)


def odd_tiles(width):
    return width if (width // 8) % 2 else width + 8


def cos_sin(rows, cols, length):
    angles = 2.0 * np.pi / length * ((rows[:, None] * cols[None, :]) % length)
    factor = 1.0 / math.sqrt(length)
    return np.cos(angles) * factor, np.sin(angles) * factor


def signed_of(width):
    return np.arange(width) - width // 2


def z_tables(count, length, planes, width):
    devices = length // planes
    cos, sin = cos_sin(signed_of(width), np.arange(length), length)
    cos = cos.reshape(width, devices, planes)
    sin = sin.reshape(width, devices, planes)
    table = np.zeros((2, count, width, devices, 2, count, planes), np.float32)
    for k in range(count):
        table[0, k, :, :, 0, k] = cos
        table[1, k, :, :, 0, k] = -sin
        table[0, k, :, :, 1, k] = sin
        table[1, k, :, :, 1, k] = cos
    size = count * 2
    return table.reshape(size * width, devices * size * planes)


def peers_of(axis):
    size = lax.axis_size(axis)
    me = lax.axis_index(axis)
    return me, [lax.rem(me + off, size) for off in range(1, size)]


def greet(axes):
    barrier = pltpu.get_barrier_semaphore()
    waits = 0
    for axis in axes:
        for peer in peers_of(axis)[1]:
            pl.semaphore_signal(barrier, inc=1, device_id={axis: peer}, device_id_type=MESH)
            waits += 1
    pl.semaphore_wait(barrier, waits)


def send_to(axis, peer, src, dst, send_sem, recv_sem):
    copy = pltpu.make_async_remote_copy(
        src_ref=src,
        dst_ref=dst,
        send_sem=send_sem,
        recv_sem=recv_sem,
        device_id={axis: peer},
        device_id_type=MESH,
    )
    copy.start()
    return copy


def arrived(axis, peer, dst, send_sem, recv_sem):
    pltpu.make_async_remote_copy(
        src_ref=dst,
        dst_ref=dst,
        send_sem=send_sem,
        recv_sem=recv_sem,
        device_id={axis: peer},
        device_id_type=MESH,
    ).wait_recv()


def packed(rows):
    half = rows.shape[1] // 2
    return jnp.concatenate([rows[:, :half], rows[:, half:]], axis=0).astype(BF16)


def unpacked(tile):
    half = tile.shape[0] // 2
    return jnp.concatenate([tile[:half], tile[half:]], axis=1)


def panel_rows(panel_ref, start):
    count = panel_ref.shape[0]
    pairs = [panel_ref[k, :, pl.ds(start, BLOCK)] for k in range(count)]
    return jnp.concatenate(
        [pair[0:1] for pair in pairs] + [pair[1:2] for pair in pairs], axis=0
    )


def one_hot(size, places):
    grid = lax.broadcasted_iota(jnp.int32, (size, places.shape[1]), 0)
    return (grid == places).astype(F32).astype(BF16)


def first_kernel(
    length, width, slot_ref, panel_ref, columns_ref, table_ref, out_ref, cols_ref, coef_ref,
    acc, stage, land, cols_land, coef_land, send_x, recv_x, send_c, recv_c, send_b, recv_b,
):
    me, others = peers_of("pw")
    here, mates = peers_of("band")
    steps = slot_ref.shape[1] // BLOCK
    lanes = land.shape[2]
    cols = acc.shape[1]
    greet(("pw", "band"))

    def pack(step, carry):
        start = pl.multiple_of(step * BLOCK, BLOCK)
        coef_land[here, step] = packed(panel_rows(panel_ref, start))
        return carry

    lax.fori_loop(0, steps, pack, 0)
    cols_land[me] = columns_ref[...]
    copies = []
    for peer in others:
        copies.append(
            send_to("pw", peer, columns_ref, cols_land.at[me], send_c.at[peer], recv_c.at[me])
        )
    for mate in mates:
        copies.append(
            send_to(
                "band", mate, coef_land.at[here], coef_land.at[here], send_b.at[mate],
                recv_b.at[here],
            )
        )
    acc[...] = jnp.zeros_like(acc)

    def scatter(step, carry):
        start = pl.multiple_of(step * BLOCK, BLOCK)
        slot = slot_ref[:, pl.ds(start, BLOCK)]
        third = lax.rem(lax.rem(slot, length) + width // 2, length)
        pick_col = one_hot(cols, slot // length)
        pick_third = one_hot(width, third)
        values = panel_rows(panel_ref, start).astype(BF16)
        spread = jnp.concatenate(
            [pick_third * values[q : q + 1] for q in range(values.shape[0])], axis=0
        )
        acc[...] += lax.dot_general(spread, pick_col, NT, preferred_element_type=F32)
        return carry

    lax.fori_loop(0, steps, scatter, 0)
    got = acc[...].astype(BF16)
    done = lax.dot_general(got, table_ref[...], TN, preferred_element_type=F32).astype(BF16)
    for d in range(land.shape[0]):
        stage[d] = done[:, d * lanes : (d + 1) * lanes]
    for peer in others:
        copies.append(
            send_to("pw", peer, stage.at[peer], land.at[me], send_x.at[peer], recv_x.at[me])
        )
    land[me] = stage[me]
    for peer in others:
        arrived("pw", peer, cols_land.at[peer], send_c.at[peer], recv_c.at[peer])
    for mate in mates:
        arrived("band", mate, coef_land.at[mate], send_b.at[mate], recv_b.at[mate])
    cols_ref[...] = cols_land[...]
    coef_ref[...] = coef_land[...]
    for peer in others:
        arrived("pw", peer, land.at[peer], send_x.at[peer], recv_x.at[peer])
    out_ref[...] = land[...]
    for copy in copies:
        copy.wait_send()


def first_part(slot, panel, columns, table, length, width, devices, mates):
    count, _, n = panel.shape
    cols = columns.shape[1]
    lanes = table.shape[1] // devices
    whole = pl.BlockSpec(memory_space=pltpu.VMEM)
    coef_shape = (mates, n // BLOCK, 4 * count, BLOCK // 2)
    dma = pltpu.SemaphoreType.DMA
    return pl.pallas_call(
        functools.partial(first_kernel, length, width),
        in_specs=[whole] * 4,
        out_specs=[whole] * 3,
        out_shape=[
            jax.ShapeDtypeStruct((devices, cols, lanes), BF16),
            jax.ShapeDtypeStruct((devices, 1, cols), jnp.int32),
            jax.ShapeDtypeStruct(coef_shape, BF16),
        ],
        scratch_shapes=[
            pltpu.VMEM((2 * count * width, cols), F32),
            pltpu.VMEM((devices, cols, lanes), BF16),
            pltpu.VMEM((devices, cols, lanes), BF16),
            pltpu.VMEM((devices, 1, cols), jnp.int32),
            pltpu.VMEM(coef_shape, BF16),
            dma((devices,)),
            dma((devices,)),
            dma((devices,)),
            dma((devices,)),
            dma((mates,)),
            dma((mates,)),
        ],
        compiler_params=pltpu.CompilerParams(
            vmem_limit_bytes=LIMIT, collective_id=1, has_side_effects=True
        ),
        name="first_part",
    )(slot, panel, columns, table)


def plane_kernel(
    wide, n_one, n_two, pos_ref, x_ref, tx_ref, ty_ref, tyb_ref, txb_ref, v_ref, out_ref,
    wave, box, mid, mid_back,
):
    total, lanes = wave.shape
    planes = v_ref.shape[0] // n_one
    sign = jnp.where(
        lax.broadcasted_iota(jnp.int32, (1, lanes), 1) < lanes // 2, -1.0, 1.0
    ).astype(F32)
    wave[...] = x_ref[...].astype(F32)
    box[...] = jnp.zeros_like(box)
    group = 16

    def put(step, carry):
        base = pl.multiple_of(step * group, group)
        tile = wave[pl.ds(base, group), :]
        for u in range(group):
            box[pl.ds(pos_ref[base + u], 1), :] = tile[u : u + 1]
        return carry

    lax.fori_loop(0, total // group, put, 0)

    def stacked(tiles):
        plain = jnp.concatenate(tiles, axis=1)
        turned = jnp.concatenate(
            [pltpu.roll(tile, lanes // 2, 1) * sign for tile in tiles], axis=1
        )
        return jnp.concatenate([plain, turned], axis=0).astype(BF16)

    def split(got):
        return [got[:, u * lanes : (u + 1) * lanes] for u in range(got.shape[1] // lanes)]

    def inverse_one(step, carry):
        tiles = [box[pl.ds(pl.multiple_of((2 * step + u) * wide, 8), wide), :] for u in range(2)]
        got = jnp.dot(tx_ref[...], stacked(tiles), preferred_element_type=F32)
        for u, tile in enumerate(split(got)):
            mid[pl.ds(2 * step + u, n_one, stride=wide), :] = tile
        return carry

    lax.fori_loop(0, wide // 2, inverse_one, 0, unroll=4)

    def both_two(step, carry):
        starts = [pl.multiple_of((2 * step + u) * wide, 8) for u in range(2)]
        tiles = [mid[pl.ds(start, wide), :] for start in starts]
        got = jnp.dot(ty_ref[...], stacked(tiles), preferred_element_type=F32)
        tiles = []
        for u, tile in enumerate(split(got)):
            local = v_ref[pl.ds(2 * step + u, planes, stride=n_one), :]
            tiles.append(tile * jnp.concatenate([local] * (lanes // planes), axis=0).T)
        back = jnp.dot(tyb_ref[...], stacked(tiles), preferred_element_type=F32)
        for u, tile in enumerate(split(back)):
            mid_back[pl.ds(starts[u], wide), :] = tile
        return carry

    lax.fori_loop(0, n_one // 2, both_two, 0, unroll=4)

    def forward_one(step, carry):
        tiles = [mid_back[pl.ds(2 * step + u, n_one, stride=wide), :] for u in range(2)]
        got = jnp.dot(txb_ref[...], stacked(tiles), preferred_element_type=F32)
        for u, tile in enumerate(split(got)):
            start = pl.multiple_of((2 * step + u) * wide, 8)
            box[pl.ds(start, wide), :] = tile
        return carry

    lax.fori_loop(0, wide // 2, forward_one, 0, unroll=4)

    def take(step, carry):
        base = pl.multiple_of(step * group, group)
        rows = [box[pl.ds(pos_ref[base + u], 1), :] for u in range(group)]
        for u in range(group):
            wave[pl.ds(base + u, 1), :] = rows[u]
        return carry

    lax.fori_loop(0, total // group, take, 0)
    out_ref[...] = wave[...].astype(BF16)


def plane_part(pos, x, tables, potential_rows, wide, n_one, n_two):
    total, lanes = x.shape
    whole = pl.BlockSpec(memory_space=pltpu.VMEM)
    return pl.pallas_call(
        functools.partial(plane_kernel, wide, n_one, n_two),
        in_specs=[pl.BlockSpec(memory_space=pltpu.SMEM)] + [whole] * 6,
        out_specs=whole,
        out_shape=jax.ShapeDtypeStruct((total, lanes), BF16),
        scratch_shapes=[
            pltpu.VMEM((total, lanes), F32),
            pltpu.VMEM((wide * wide, lanes), F32),
            pltpu.VMEM((n_one * wide, lanes), F32),
            pltpu.VMEM((n_one * wide, lanes), F32),
        ],
        compiler_params=pltpu.CompilerParams(vmem_limit_bytes=LIMIT),
        name="plane_part",
    )(pos, x, *tables, potential_rows)


def last_kernel(
    lengths, width, groups, slot_ref, panel_ref, x_ref, table_ref, marks_ref, coef_ref, slab_ref,
    out_ref, home, held, app, slab_in, slab_rows, acc_h, acc_m, terms, part, parts,
    slab_sem, send_x, recv_x, send_b, recv_b, send_p, recv_p,
):
    n_one, n_two, length = lengths
    me, others = peers_of("pw")
    here, mates = peers_of("band")
    bands = len(mates) + 1
    size = 2 * panel_ref.shape[0]
    body = size * width
    cols = held.shape[1]
    steps = slot_ref.shape[1] // BLOCK
    each = steps // groups
    fetch = pltpu.make_async_copy(slab_ref, slab_in, slab_sem)
    fetch.start()
    greet(("pw", "band"))
    copies = [
        send_to("pw", peer, x_ref.at[peer], home.at[me], send_x.at[peer], recv_x.at[me])
        for peer in others
    ]
    home[me] = x_ref[me]
    held[body:, :] = marks_ref[...]
    acc_h[...] = jnp.zeros_like(acc_h)
    acc_m[...] = jnp.zeros_like(acc_m)
    fetch.wait()

    def project(acc, slab_tile, ref, step):
        right = jnp.concatenate([unpacked(ref[b, step]) for b in range(bands)], axis=0)
        acc[...] += lax.dot_general(slab_tile, right, NT, preferred_element_type=F32)

    def margin(step, carry):
        start = pl.multiple_of(step * BLOCK, BLOCK)
        tile = slab_in[:, :, pl.ds(start, BLOCK)].reshape(slab_rows.shape[0], BLOCK)
        slab_rows[:, pl.ds(start, BLOCK)] = tile
        project(acc_m, tile, coef_ref, step)
        return carry

    lax.fori_loop(0, steps, margin, 0)
    for peer in others:
        arrived("pw", peer, home.at[peer], send_x.at[peer], recv_x.at[peer])
    x = jnp.concatenate([home[d] for d in range(home.shape[0])], axis=1)
    held[:body, :] = lax.dot_general(
        table_ref[...], x, NT, preferred_element_type=F32
    ).astype(BF16)

    def gather(step, carry):
        start = pl.multiple_of(step * BLOCK, BLOCK)
        slot = slot_ref[:, pl.ds(start, BLOCK)]
        third = lax.rem(slot, length)
        place = lax.rem(third + width // 2, length)
        pick_col = one_hot(cols, slot // length)
        at_third = lax.broadcasted_iota(jnp.int32, (width, BLOCK), 0) == place
        got = jnp.dot(held[...], pick_col, preferred_element_type=F32)
        f_one = got[body : body + 1] * (2.0 / n_one)
        f_two = got[body + 1 : body + 2] * (2.0 / n_two)
        signed = jnp.where(third < length // 2, third, third - length)
        f_three = signed.astype(F32) * (2.0 / length)
        kinetic = 0.5 * (f_one * f_one + f_two * f_two + f_three * f_three)
        picked = jnp.concatenate(
            [
                jnp.sum(
                    jnp.where(at_third, got[q * width : (q + 1) * width], 0.0),
                    axis=0,
                    keepdims=True,
                )
                for q in range(size)
            ],
            axis=0,
        )
        app[here, step] = packed(kinetic * panel_rows(panel_ref, start) + picked)
        return carry

    for g in range(groups):
        lax.fori_loop(g * each, (g + 1) * each, gather, 0)
        span = pl.ds(g * each, each)
        for mate in mates:
            copies.append(
                send_to(
                    "band", mate, app.at[here, span], app.at[here, span],
                    send_b.at[mate, g], recv_b.at[here, g],
                )
            )

    def hamiltonian(step, carry):
        start = pl.multiple_of(step * BLOCK, BLOCK)
        project(acc_h, slab_rows[:, pl.ds(start, BLOCK)], app, step)
        return carry

    for g in range(groups):
        span = pl.ds(g * each, each)
        for mate in mates:
            arrived("band", mate, app.at[mate, span], send_b.at[mate, g], recv_b.at[mate, g])
        lax.fori_loop(g * each, (g + 1) * each, hamiltonian, 0)

    terms[...] = jnp.concatenate([acc_h[...], acc_m[...]], axis=1)
    rows = terms.shape[0] // 2
    real_rows = terms[pl.ds(0, rows, stride=2), :].T
    imag_rows = terms[pl.ds(1, rows, stride=2), :].T

    def pick(value, kind, which):
        first = kind * bands * size + which * (size // 2)
        return jnp.concatenate(
            [value[first + b * size : first + b * size + size // 2] for b in range(bands)], axis=0
        )

    pieces = []
    for kind in range(2):
        pieces.append(pick(real_rows, kind, 0) + pick(imag_rows, kind, 1))
        pieces.append(pick(real_rows, kind, 1) - pick(imag_rows, kind, 0))
    part[...] = jnp.concatenate(pieces, axis=0)
    share = out_ref.shape[0]

    def block_of(index):
        return pl.ds(pl.multiple_of(index * share, share), share)

    for peer in others:
        copies.append(
            send_to(
                "pw", peer, part.at[block_of(peer)], parts.at[me], send_p.at[peer], recv_p.at[me]
            )
        )
    parts[me] = part[block_of(me), :]
    for peer in others:
        arrived("pw", peer, parts.at[peer], send_p.at[peer], recv_p.at[peer])
    total = parts[0]
    for d in range(1, parts.shape[0]):
        total = total + parts[d]
    out_ref[...] = total
    for copy in copies:
        copy.wait_send()


def last_part(slot, panel, x, table, marks, coef, slab, lengths, width):
    devices, cols, lanes = x.shape
    count, _, n = panel.shape
    mates = coef.shape[0]
    size = 2 * count
    rows = slab.shape[0]
    groups = 3 if (n // BLOCK) % 3 == 0 else 1
    share = 2 * mates * size // devices
    whole = pl.BlockSpec(memory_space=pltpu.VMEM)
    dma = pltpu.SemaphoreType.DMA
    return pl.pallas_call(
        functools.partial(last_kernel, lengths, width, groups),
        in_specs=[whole] * 6 + [pl.BlockSpec(memory_space=pl.ANY)],
        out_specs=whole,
        out_shape=jax.ShapeDtypeStruct((share, rows), F32),
        scratch_shapes=[
            pltpu.VMEM((devices, cols, lanes), BF16),
            pltpu.VMEM((size * width + marks.shape[0], cols), BF16),
            pltpu.VMEM(coef.shape, BF16),
            pltpu.VMEM(slab.shape, BF16),
            pltpu.VMEM((2 * rows, n), BF16),
            pltpu.VMEM((2 * rows, mates * size), F32),
            pltpu.VMEM((2 * rows, mates * size), F32),
            pltpu.VMEM((2 * rows, 2 * mates * size), F32),
            pltpu.VMEM((2 * mates * size, rows), F32),
            pltpu.VMEM((devices, share, rows), F32),
            dma,
            dma((devices,)),
            dma((devices,)),
            dma((mates, groups)),
            dma((mates, groups)),
            dma((devices,)),
            dma((devices,)),
        ],
        compiler_params=pltpu.CompilerParams(
            vmem_limit_bytes=LIMIT, collective_id=2, has_side_effects=True
        ),
        name="last_part",
    )(slot, panel, x, table, marks, coef, slab)


def signed_index(index, length):
    return jnp.where(index < length // 2, index, index - length)


def per_device(slab, panel, potential, pw_slot, columns):
    devices = lax.axis_size("pw")
    mates = lax.axis_size("band")
    planes, n_one, n_two = potential.shape
    length = planes * devices
    cols = columns.shape[0]
    count = panel.shape[0]
    n = panel.shape[2]
    lanes = 2 * count * planes

    square = disk_square(n_one, n_two, cols * devices)
    wide = odd_tiles(window(math.isqrt(square), 8, max(n_one, n_two)))
    reach = math.isqrt(square + (-(-n // (2 * cols)) + 2) ** 2) + 1
    width = window(reach, 16, length)

    ztab = jnp.asarray(z_tables(count, length, planes, width), BF16)
    cy, sy = cos_sin(np.arange(n_two), signed_of(wide), n_two)
    cx, sx = cos_sin(np.arange(n_one), signed_of(wide), n_one)
    tables = [
        np.concatenate([cx, sx], axis=1),
        np.concatenate([cy, sy], axis=1),
        np.concatenate([cy.T, -sy.T], axis=1),
        np.concatenate([cx.T, -sx.T], axis=1),
    ]
    tables = [jnp.asarray(t, BF16) for t in tables]

    slot = pw_slot.reshape(1, n)
    mine = jnp.stack(
        [signed_index(columns // n_two, n_one), signed_index(columns % n_two, n_two)], axis=0
    )
    marks = jnp.concatenate([mine, jnp.zeros((14, cols), jnp.int32)], axis=0).astype(BF16)

    there, every_column, coef = first_part(
        slot, panel, columns.reshape(1, cols), ztab, length, width, devices, mates
    )
    every_column = every_column.reshape(devices * cols)
    place_one = signed_index(every_column // n_two, n_one) + wide // 2
    place_two = signed_index(every_column % n_two, n_two) + wide // 2
    worked = plane_part(
        place_two * wide + place_one,
        there.reshape(devices * cols, lanes),
        tables,
        potential.reshape(planes * n_one, n_two),
        wide,
        n_one,
        n_two,
    )
    out = last_part(
        slot,
        panel,
        worked.reshape(devices, cols, lanes),
        ztab,
        marks,
        coef,
        slab,
        (n_one, n_two, length),
        width,
    )
    return out.T


def solution(mesh):
    in_specs = (P("band", None, "pw"), P("band", None, "pw"), P("pw", None, None), P("pw"), P("pw"))
    out_specs = P("band", "pw")
    return jax.shard_map(
        per_device, mesh=mesh, in_specs=in_specs, out_specs=out_specs, check_vma=False
    )
```

```python
import functools
import math

import jax
import jax.numpy as jnp
import numpy as np
from jax import lax
from jax.experimental import pallas as pl
from jax.experimental.pallas import tpu as pltpu
from jax.sharding import PartitionSpec as P

F32 = jnp.float32
BF16 = jnp.bfloat16
NT = (((1,), (1,)), ((), ()))
TN = (((0,), (0,)), ((), ()))
MESH = pl.DeviceIdType.MESH
BLOCK = 1024
LIMIT = 56 * 1024 * 1024


def round_up(value, step):
    return -(-value // step) * step


def disk_square(first_len, second_len, count):
    one = np.arange(first_len) - first_len // 2
    two = np.arange(second_len) - second_len // 2
    return int(np.sort((one[:, None] ** 2 + two[None, :] ** 2).ravel())[count - 1])


def window(half, step, length):
    return min(round_up(2 * (half + 1), step), length)


def odd_tiles(width):
    return width if (width // 8) % 2 else width + 8


def cos_sin(rows, cols, length):
    angles = 2.0 * np.pi / length * ((rows[:, None] * cols[None, :]) % length)
    factor = 1.0 / math.sqrt(length)
    return np.cos(angles) * factor, np.sin(angles) * factor


def signed_of(width):
    return np.arange(width) - width // 2


def z_tables(count, length, planes, width):
    devices = length // planes
    cos, sin = cos_sin(signed_of(width), np.arange(length), length)
    cos = cos.reshape(width, devices, planes)
    sin = sin.reshape(width, devices, planes)
    table = np.zeros((2, count, width, devices, 2, count, planes), np.float32)
    for k in range(count):
        table[0, k, :, :, 0, k] = cos
        table[1, k, :, :, 0, k] = -sin
        table[0, k, :, :, 1, k] = sin
        table[1, k, :, :, 1, k] = cos
    size = count * 2
    return table.reshape(size * width, devices * size * planes)


def peers_of(axis):
    size = lax.axis_size(axis)
    me = lax.axis_index(axis)
    offs = sorted(range(1, size), key=lambda off: abs(2 * off - size))
    return me, [lax.rem(me + off, size) for off in offs]


def greet(axes):
    barrier = pltpu.get_barrier_semaphore()
    waits = 0
    for axis in axes:
        for peer in peers_of(axis)[1]:
            pl.semaphore_signal(barrier, inc=1, device_id={axis: peer}, device_id_type=MESH)
            waits += 1
    pl.semaphore_wait(barrier, waits)


def send_to(axis, peer, src, dst, send_sem, recv_sem):
    copy = pltpu.make_async_remote_copy(
        src_ref=src,
        dst_ref=dst,
        send_sem=send_sem,
        recv_sem=recv_sem,
        device_id={axis: peer},
        device_id_type=MESH,
    )
    copy.start()
    return copy


def arrived(axis, peer, dst, send_sem, recv_sem):
    pltpu.make_async_remote_copy(
        src_ref=dst,
        dst_ref=dst,
        send_sem=send_sem,
        recv_sem=recv_sem,
        device_id={axis: peer},
        device_id_type=MESH,
    ).wait_recv()


def packed(rows):
    pieces = 16 // rows.shape[0]
    lanes = rows.shape[1] // pieces
    return jnp.concatenate(
        [rows[:, p * lanes : (p + 1) * lanes] for p in range(pieces)], axis=0
    ).astype(BF16)


def unpacked(tile, rows):
    tile = tile.astype(F32)
    return jnp.concatenate(
        [tile[p * rows : (p + 1) * rows] for p in range(tile.shape[0] // rows)], axis=1
    )


def half_rows(panel_ref, half, start):
    bands = panel_ref.shape[0] // 2
    pairs = [panel_ref[half * bands + k, :, pl.ds(start, BLOCK)] for k in range(bands)]
    return jnp.concatenate(
        [pair[0:1] for pair in pairs] + [pair[1:2] for pair in pairs], axis=0
    )


def all_rows(panel_ref, start):
    return jnp.concatenate([half_rows(panel_ref, half, start) for half in range(2)], axis=0)


def signed_index(index, length):
    return jnp.where(index < length // 2, index, index - length)


def fold_slab(slab_in, slab_rows, step, first):
    start = pl.multiple_of(step * BLOCK, BLOCK)
    tile = slab_in[:, :, pl.ds(pl.multiple_of((step - first) * BLOCK, BLOCK), BLOCK)]
    tile = tile.reshape(slab_rows.shape[0], BLOCK)
    slab_rows[:, pl.ds(start, BLOCK)] = tile
    return tile


def add_product(acc, slab_tile, pieces):
    right = jnp.concatenate(pieces, axis=0).astype(BF16)
    acc[...] += lax.dot_general(slab_tile, right, NT, preferred_element_type=F32)


def one_hot(size, places):
    grid = lax.broadcasted_iota(jnp.int32, (size, places.shape[1]), 0)
    return (grid == places).astype(F32).astype(BF16)


def first_kernel(
    sizes, wide, width, slot_ref, panel_ref, columns_ref, table_ref, slab_ref,
    out_ref, pos_ref, coef_ref, acc_ref, rows_ref,
    acc, picks, thirds, stage, land, pos_mine, pos_land, coef_land, slab_in, slab_rows,
    slab_sem, rows_sem, send_x, recv_x, send_c, recv_c, send_b, recv_b,
):
    n_one, n_two, length = sizes
    me, others = peers_of("pw")
    here, mates = peers_of("band")
    steps = slot_ref.shape[1] // BLOCK
    cols = acc.shape[1]
    side = land.shape[3] // 2
    size = 2 * panel_ref.shape[0]
    fetch = pltpu.make_async_copy(
        slab_ref.at[:, :, pl.ds(0, slab_in.shape[2])], slab_in, slab_sem
    )
    fetch.start()
    greet(("pw", "band"))

    def pack(step, carry):
        start = pl.multiple_of(step * BLOCK, BLOCK)
        coef_land[here, step] = packed(all_rows(panel_ref, start))
        return carry

    lax.fori_loop(0, steps, pack, 0)
    column = columns_ref[...]
    place_one = signed_index(column // n_two, n_one) + wide // 2
    place_two = signed_index(lax.rem(column, n_two), n_two) + wide // 2
    pos_mine[...] = place_two * wide + place_one
    pos_land[me] = pos_mine[...]
    copies = []
    for peer in others:
        copies.append(
            send_to("pw", peer, pos_mine, pos_land.at[me], send_c.at[peer], recv_c.at[me])
        )
    for mate in mates:
        copies.append(
            send_to(
                "band", mate, coef_land.at[here], coef_land.at[here], send_b.at[mate],
                recv_b.at[here],
            )
        )

    for half in range(2):
        acc[...] = jnp.zeros_like(acc)

        def scatter(step, carry):
            start = pl.multiple_of(step * BLOCK, BLOCK)
            if half == 0:
                slot = slot_ref[:, pl.ds(start, BLOCK)]
                third = lax.rem(lax.rem(slot, length) + width // 2, length)
                pick_col = one_hot(cols, slot // length)
                pick_third = one_hot(width, third)
                picks[step] = pick_col
                thirds[step] = pick_third
            else:
                pick_col = picks[step]
                pick_third = thirds[step]
            values = half_rows(panel_ref, half, start).astype(BF16)
            spread = jnp.concatenate(
                [pick_third * values[q : q + 1] for q in range(values.shape[0])], axis=0
            )
            acc[...] += lax.dot_general(spread, pick_col, NT, preferred_element_type=F32)
            return carry

        lax.fori_loop(0, steps, scatter, 0)
        got = acc[...].astype(BF16)
        done = lax.dot_general(got, table_ref[...], TN, preferred_element_type=F32)
        for d in range(land.shape[0]):
            piece = done[:, d * side : (d + 1) * side]
            stage[half, d] = jnp.concatenate(
                [piece[: cols // 2], piece[cols // 2 :]], axis=1
            ).astype(BF16)
        for peer in others:
            copies.append(
                send_to(
                    "pw", peer, stage.at[half, peer], land.at[me, half],
                    send_x.at[peer, half], recv_x.at[me, half],
                )
            )
        land[me, half] = stage[half, me]

    for mate in mates:
        arrived("band", mate, coef_land.at[mate], send_b.at[mate], recv_b.at[mate])
    fetch.wait()
    acc_ref[...] = jnp.zeros_like(acc_ref)

    def margin(step, carry):
        tile = fold_slab(slab_in, slab_rows, step, 0)
        add_product(
            acc_ref, tile, [unpacked(coef_land[b, step], size) for b in range(len(mates) + 1)]
        )
        return carry

    lax.fori_loop(0, slab_in.shape[2] // BLOCK, margin, 0)
    keep = pltpu.make_async_copy(slab_rows, rows_ref, rows_sem)
    keep.start()
    for peer in others:
        arrived("pw", peer, pos_land.at[peer], send_c.at[peer], recv_c.at[peer])
    pos_ref[...] = pos_land[...]
    coef_ref[...] = coef_land[...]
    for half in range(2):
        for peer in others:
            arrived(
                "pw", peer, land.at[peer, half], send_x.at[peer, half], recv_x.at[peer, half]
            )
    out_ref[...] = land[...]
    for copy in copies:
        copy.wait_send()
    keep.wait()


def first_part(slot, panel, columns, table, slab, sizes, wide, width, devices, mates):
    count, _, n = panel.shape
    cols = columns.shape[1]
    lanes = 2 * (table.shape[1] // devices)
    steps = n // BLOCK
    early = (steps // 2) * BLOCK
    rows = 2 * slab.shape[0]
    whole = pl.BlockSpec(memory_space=pltpu.VMEM)
    anywhere = pl.BlockSpec(memory_space=pl.ANY)
    coef_shape = (mates, steps, 16, BLOCK * count // 8)
    wave_shape = (devices, 2, cols // 2, lanes)
    dma = pltpu.SemaphoreType.DMA
    return pl.pallas_call(
        functools.partial(first_kernel, sizes, wide, width),
        in_specs=[whole] * 4 + [anywhere],
        out_specs=[whole] * 4 + [anywhere],
        out_shape=[
            jax.ShapeDtypeStruct(wave_shape, BF16),
            jax.ShapeDtypeStruct((devices, 1, cols), jnp.int32),
            jax.ShapeDtypeStruct(coef_shape, BF16),
            jax.ShapeDtypeStruct((rows, 2 * count * mates), F32),
            jax.ShapeDtypeStruct((rows, early), BF16),
        ],
        scratch_shapes=[
            pltpu.VMEM((count * width, cols), F32),
            pltpu.VMEM((steps, cols, BLOCK), BF16),
            pltpu.VMEM((steps, width, BLOCK), BF16),
            pltpu.VMEM((2, devices, cols // 2, lanes), BF16),
            pltpu.VMEM(wave_shape, BF16),
            pltpu.VMEM((1, cols), jnp.int32),
            pltpu.VMEM((devices, 1, cols), jnp.int32),
            pltpu.VMEM(coef_shape, BF16),
            pltpu.VMEM((slab.shape[0], 2, early), BF16),
            pltpu.VMEM((rows, early), BF16),
            dma,
            dma,
            dma((devices, 2)),
            dma((devices, 2)),
            dma((devices,)),
            dma((devices,)),
            dma((mates,)),
            dma((mates,)),
        ],
        compiler_params=pltpu.CompilerParams(
            vmem_limit_bytes=LIMIT, collective_id=1, has_side_effects=True
        ),
        name="first_part",
    )(slot, panel, columns, table, slab)


def plane_kernel(
    wide, n_one, n_two, pos_ref, x_ref, tx_ref, ty_ref, tyb_ref, txb_ref, v_ref, out_ref,
    wave, box, mid, mid_back,
):
    total, lanes = wave.shape
    planes = v_ref.shape[0] // n_one
    sign = jnp.where(
        lax.broadcasted_iota(jnp.int32, (1, lanes), 1) < lanes // 2, -1.0, 1.0
    ).astype(F32)
    devices, _, rows, _ = x_ref.shape
    piece = lanes // 4

    def quarters(tile):
        return [tile[:, p * piece : (p + 1) * piece] for p in range(4)]

    def unfold(d, carry):
        low = quarters(x_ref[d, 0].astype(F32))
        high = quarters(x_ref[d, 1].astype(F32))
        for side in range(2):
            base = pl.multiple_of((2 * d + side) * rows, rows)
            wave[pl.ds(base, rows), :] = jnp.concatenate(
                [low[2 * side], high[2 * side], low[2 * side + 1], high[2 * side + 1]], axis=1
            )
        return carry

    lax.fori_loop(0, devices, unfold, 0)
    box[...] = jnp.zeros_like(box)
    group = 16
    per = 2 * rows // group

    def put(step, carry):
        base = pl.multiple_of(step * group, group)
        tile = wave[pl.ds(base, group), :]
        d = step // per
        start = (step - d * per) * group
        for u in range(group):
            box[pl.ds(pos_ref[d, 0, start + u], 1), :] = tile[u : u + 1]
        return carry

    lax.fori_loop(0, total // group, put, 0)

    def stacked(tiles):
        plain = jnp.concatenate(tiles, axis=1)
        turned = jnp.concatenate(
            [pltpu.roll(tile, lanes // 2, 1) * sign for tile in tiles], axis=1
        )
        return jnp.concatenate([plain, turned], axis=0).astype(BF16)

    def split(got):
        return [got[:, u * lanes : (u + 1) * lanes] for u in range(got.shape[1] // lanes)]

    def inverse_one(step, carry):
        tiles = [box[pl.ds(pl.multiple_of((2 * step + u) * wide, 8), wide), :] for u in range(2)]
        got = jnp.dot(tx_ref[...], stacked(tiles), preferred_element_type=F32)
        for u, tile in enumerate(split(got)):
            mid[pl.ds(2 * step + u, n_one, stride=wide), :] = tile
        return carry

    lax.fori_loop(0, wide // 2, inverse_one, 0, unroll=4)

    def both_two(step, carry):
        starts = [pl.multiple_of((2 * step + u) * wide, 8) for u in range(2)]
        tiles = [mid[pl.ds(start, wide), :] for start in starts]
        got = jnp.dot(ty_ref[...], stacked(tiles), preferred_element_type=F32)
        tiles = []
        for u, tile in enumerate(split(got)):
            local = v_ref[pl.ds(2 * step + u, planes, stride=n_one), :]
            tiles.append(tile * jnp.concatenate([local] * (lanes // planes), axis=0).T)
        back = jnp.dot(tyb_ref[...], stacked(tiles), preferred_element_type=F32)
        for u, tile in enumerate(split(back)):
            mid_back[pl.ds(starts[u], wide), :] = tile
        return carry

    lax.fori_loop(0, n_one // 2, both_two, 0, unroll=4)

    def forward_one(step, carry):
        tiles = [mid_back[pl.ds(2 * step + u, n_one, stride=wide), :] for u in range(2)]
        got = jnp.dot(txb_ref[...], stacked(tiles), preferred_element_type=F32)
        for u, tile in enumerate(split(got)):
            start = pl.multiple_of((2 * step + u) * wide, 8)
            box[pl.ds(start, wide), :] = tile
        return carry

    lax.fori_loop(0, wide // 2, forward_one, 0, unroll=4)

    def take(step, carry):
        base = pl.multiple_of(step * group, group)
        d = step // per
        start = (step - d * per) * group
        taken = [box[pl.ds(pos_ref[d, 0, start + u], 1), :] for u in range(group)]
        for u in range(group):
            wave[pl.ds(base + u, 1), :] = taken[u]
        return carry

    lax.fori_loop(0, total // group, take, 0)

    def fold(d, carry):
        sides = [
            quarters(wave[pl.ds(pl.multiple_of((2 * d + side) * rows, rows), rows), :])
            for side in range(2)
        ]
        for half in range(2):
            out_ref[d, half] = jnp.concatenate(
                [sides[side][half + 2 * which] for side in range(2) for which in range(2)], axis=1
            ).astype(BF16)
        return carry

    lax.fori_loop(0, devices, fold, 0)


def plane_part(pos, x, tables, potential_rows, wide, n_one, n_two):
    devices, _, rows, lanes = x.shape
    total = 2 * devices * rows
    whole = pl.BlockSpec(memory_space=pltpu.VMEM)
    return pl.pallas_call(
        functools.partial(plane_kernel, wide, n_one, n_two),
        in_specs=[pl.BlockSpec(memory_space=pltpu.SMEM)] + [whole] * 6,
        out_specs=whole,
        out_shape=jax.ShapeDtypeStruct(x.shape, BF16),
        scratch_shapes=[
            pltpu.VMEM((total, lanes), F32),
            pltpu.VMEM((wide * wide, lanes), F32),
            pltpu.VMEM((n_one * wide, lanes), F32),
            pltpu.VMEM((n_one * wide, lanes), F32),
        ],
        compiler_params=pltpu.CompilerParams(vmem_limit_bytes=LIMIT),
        name="plane_part",
    )(pos, x, *tables, potential_rows)


def last_kernel(
    sizes, width, groups, slot_ref, panel_ref, columns_ref, x_ref, table_ref, coef_ref, acc_ref,
    rows_ref, slab_ref, out_ref,
    home, held, picks, kinetics, app, slab_in, slab_rows, acc_h, acc_m, terms, part, parts,
    slab_sem, rows_sem, send_x, recv_x, send_b, recv_b, send_p, recv_p,
):
    n_one, n_two, length = sizes
    me, others = peers_of("pw")
    here, mates = peers_of("band")
    bands = len(mates) + 1
    count = panel_ref.shape[0]
    size = 2 * count
    body = count * width
    cols = held.shape[1]
    steps = slot_ref.shape[1] // BLOCK
    each = steps // groups
    early = rows_ref.shape[1]
    fetch = pltpu.make_async_copy(
        slab_ref.at[:, :, pl.ds(early, slab_in.shape[2])], slab_in, slab_sem
    )
    fetch.start()
    again = pltpu.make_async_copy(rows_ref, slab_rows.at[:, pl.ds(0, early)], rows_sem)
    again.start()
    greet(("pw", "band"))
    copies = []
    for half in range(2):
        for peer in others:
            copies.append(
                send_to(
                    "pw", peer, x_ref.at[peer, half], home.at[me, half],
                    send_x.at[peer, half], recv_x.at[me, half],
                )
            )
    home[me] = x_ref[me]
    column = columns_ref[...]
    held[body:, :] = jnp.concatenate(
        [
            signed_index(column // n_two, n_one),
            signed_index(lax.rem(column, n_two), n_two),
            jnp.zeros((14, cols), jnp.int32),
        ],
        axis=0,
    ).astype(F32).astype(BF16)
    acc_h[...] = jnp.zeros_like(acc_h)
    acc_m[...] = acc_ref[...]
    fetch.wait()

    def margin(step, carry):
        tile = fold_slab(slab_in, slab_rows, step, early // BLOCK)
        add_product(acc_m, tile, [unpacked(coef_ref[b, step], size) for b in range(bands)])
        return carry

    lax.fori_loop(early // BLOCK, steps, margin, 0)
    again.wait()

    for half in range(2):
        for peer in others:
            arrived(
                "pw", peer, home.at[peer, half], send_x.at[peer, half], recv_x.at[peer, half]
            )
        pieces = [home[d, half].astype(F32) for d in range(home.shape[0])]
        side = home.shape[3] // 2
        x = jnp.concatenate(
            [
                jnp.concatenate([piece[:, :side] for piece in pieces], axis=1),
                jnp.concatenate([piece[:, side:] for piece in pieces], axis=1),
            ],
            axis=0,
        ).astype(BF16)
        held[:body, :] = lax.dot_general(
            table_ref[...], x, NT, preferred_element_type=F32
        ).astype(BF16)

        def gather(step, carry):
            start = pl.multiple_of(step * BLOCK, BLOCK)
            slot = slot_ref[:, pl.ds(start, BLOCK)]
            third = lax.rem(slot, length)
            place = lax.rem(third + width // 2, length)
            at_third = lax.broadcasted_iota(jnp.int32, (width, BLOCK), 0) == place
            if half == 0:
                pick_col = one_hot(cols, slot // length)
                picks[step] = pick_col
                got = jnp.dot(held[...], pick_col, preferred_element_type=F32)
                f_one = got[body : body + 1] * (2.0 / n_one)
                f_two = got[body + 1 : body + 2] * (2.0 / n_two)
                f_three = signed_index(third, length).astype(F32) * (2.0 / length)
                kinetic = 0.5 * (f_one * f_one + f_two * f_two + f_three * f_three)
                kinetics[:, pl.ds(start, BLOCK)] = kinetic
            else:
                got = jnp.dot(held[:body, :], picks[step], preferred_element_type=F32)
                kinetic = kinetics[:, pl.ds(start, BLOCK)]
            picked = jnp.concatenate(
                [
                    jnp.sum(
                        jnp.where(at_third, got[q * width : (q + 1) * width], 0.0),
                        axis=0,
                        keepdims=True,
                    )
                    for q in range(count)
                ],
                axis=0,
            )
            app[here, half, step] = packed(kinetic * half_rows(panel_ref, half, start) + picked)
            return carry

        for g in range(groups):
            lax.fori_loop(g * each, (g + 1) * each, gather, 0)
            span = pl.ds(g * each, each)
            for mate in mates:
                copies.append(
                    send_to(
                        "band", mate, app.at[here, half, span], app.at[here, half, span],
                        send_b.at[mate, half, g], recv_b.at[here, half, g],
                    )
                )

    def hamiltonian(step, carry):
        start = pl.multiple_of(step * BLOCK, BLOCK)
        add_product(
            acc_h,
            slab_rows[:, pl.ds(start, BLOCK)],
            [unpacked(app[b, half, step], count) for b in range(bands) for half in range(2)],
        )
        return carry

    for g in range(groups):
        span = pl.ds(g * each, each)
        for mate in mates:
            for half in range(2):
                arrived(
                    "band", mate, app.at[mate, half, span], send_b.at[mate, half, g],
                    recv_b.at[mate, half, g],
                )
        lax.fori_loop(g * each, (g + 1) * each, hamiltonian, 0)

    terms[...] = jnp.concatenate([acc_h[...], acc_m[...]], axis=1)
    rows = terms.shape[0] // 2
    real_rows = terms[pl.ds(0, rows, stride=2), :].T
    imag_rows = terms[pl.ds(1, rows, stride=2), :].T

    def pick(value, kind, which):
        first = kind * bands * size + which * (count // 2)
        return jnp.concatenate(
            [value[first + b * count : first + b * count + count // 2] for b in range(2 * bands)],
            axis=0,
        )

    pieces = []
    for kind in range(2):
        pieces.append(pick(real_rows, kind, 0) + pick(imag_rows, kind, 1))
        pieces.append(pick(real_rows, kind, 1) - pick(imag_rows, kind, 0))
    part[...] = jnp.concatenate(pieces, axis=0)
    share = out_ref.shape[0]

    def block_of(index):
        return pl.ds(pl.multiple_of(index * share, share), share)

    for peer in others:
        copies.append(
            send_to(
                "pw", peer, part.at[block_of(peer)], parts.at[me], send_p.at[peer], recv_p.at[me]
            )
        )
    parts[me] = part[block_of(me), :]
    for peer in others:
        arrived("pw", peer, parts.at[peer], send_p.at[peer], recv_p.at[peer])
    total = parts[0]
    for d in range(1, parts.shape[0]):
        total = total + parts[d]
    out_ref[...] = total
    for copy in copies:
        copy.wait_send()


def last_part(slot, panel, columns, x, table, coef, margin, slab_rows, slab, sizes, width):
    devices = x.shape[0]
    cols = columns.shape[1]
    count, _, n = panel.shape
    mates, steps = coef.shape[:2]
    size = 2 * count
    rows = slab.shape[0]
    groups = 3 if steps % 3 == 0 else 1
    share = 2 * mates * size // devices
    whole = pl.BlockSpec(memory_space=pltpu.VMEM)
    anywhere = pl.BlockSpec(memory_space=pl.ANY)
    dma = pltpu.SemaphoreType.DMA
    return pl.pallas_call(
        functools.partial(last_kernel, sizes, width, groups),
        in_specs=[whole] * 7 + [anywhere] * 2,
        out_specs=whole,
        out_shape=jax.ShapeDtypeStruct((share, rows), F32),
        scratch_shapes=[
            pltpu.VMEM(x.shape, BF16),
            pltpu.VMEM((count * width + 16, cols), BF16),
            pltpu.VMEM((steps, cols, BLOCK), BF16),
            pltpu.VMEM((1, n), F32),
            pltpu.VMEM((mates, 2, steps, 16, BLOCK * count // 16), BF16),
            pltpu.VMEM((rows, 2, n - slab_rows.shape[1]), BF16),
            pltpu.VMEM((2 * rows, n), BF16),
            pltpu.VMEM((2 * rows, mates * size), F32),
            pltpu.VMEM((2 * rows, mates * size), F32),
            pltpu.VMEM((2 * rows, 2 * mates * size), F32),
            pltpu.VMEM((2 * mates * size, rows), F32),
            pltpu.VMEM((devices, share, rows), F32),
            dma,
            dma,
            dma((devices, 2)),
            dma((devices, 2)),
            dma((mates, 2, groups)),
            dma((mates, 2, groups)),
            dma((devices,)),
            dma((devices,)),
        ],
        compiler_params=pltpu.CompilerParams(
            vmem_limit_bytes=LIMIT, collective_id=2, has_side_effects=True
        ),
        name="last_part",
    )(slot, panel, columns, x, table, coef, margin, slab_rows, slab)


def per_device(slab, panel, potential, pw_slot, columns):
    devices = lax.axis_size("pw")
    mates = lax.axis_size("band")
    planes, n_one, n_two = potential.shape
    length = planes * devices
    cols = columns.shape[0]
    count = panel.shape[0]
    n = panel.shape[2]

    square = disk_square(n_one, n_two, cols * devices)
    wide = odd_tiles(window(math.isqrt(square), 8, max(n_one, n_two)))
    reach = math.isqrt(square + (-(-n // (2 * cols)) + 2) ** 2) + 1
    width = window(reach, 16, length)

    ztab = jnp.asarray(z_tables(count // 2, length, planes, width), BF16)
    cy, sy = cos_sin(np.arange(n_two), signed_of(wide), n_two)
    cx, sx = cos_sin(np.arange(n_one), signed_of(wide), n_one)
    tables = [
        np.concatenate([cx, sx], axis=1),
        np.concatenate([cy, sy], axis=1),
        np.concatenate([cy.T, -sy.T], axis=1),
        np.concatenate([cx.T, -sx.T], axis=1),
    ]
    tables = [jnp.asarray(t, BF16) for t in tables]

    slot = pw_slot.reshape(1, n)
    owned = columns.reshape(1, cols)
    sizes = (n_one, n_two, length)
    there, pos, coef, margin, slab_rows = first_part(
        slot, panel, owned, ztab, slab, sizes, wide, width, devices, mates
    )
    worked = plane_part(
        pos, there, tables, potential.reshape(planes * n_one, n_two), wide, n_one, n_two
    )
    out = last_part(
        slot, panel, owned, worked, ztab, coef, margin, slab_rows, slab, sizes, width
    )
    return out.T


def solution(mesh):
    in_specs = (P("band", None, "pw"), P("band", None, "pw"), P("pw", None, None), P("pw"), P("pw"))
    out_specs = P("band", "pw")
    return jax.shard_map(
        per_device, mesh=mesh, in_specs=in_specs, out_specs=out_specs, check_vma=False
    )
```

```python
import functools
import math

import jax
import jax.numpy as jnp
import numpy as np
from jax import lax
from jax.experimental import pallas as pl
from jax.experimental.pallas import tpu as pltpu
from jax.sharding import PartitionSpec as P

F32 = jnp.float32
BF16 = jnp.bfloat16
NT = (((1,), (1,)), ((), ()))
TN = (((0,), (0,)), ((), ()))
MESH = pl.DeviceIdType.MESH
BLOCK = 1024
LIMIT = 56 * 1024 * 1024


def round_up(value, step):
    return -(-value // step) * step


def disk_square(first_len, second_len, count):
    one = np.arange(first_len) - first_len // 2
    two = np.arange(second_len) - second_len // 2
    return int(np.sort((one[:, None] ** 2 + two[None, :] ** 2).ravel())[count - 1])


def window(half, step, length):
    return min(round_up(2 * (half + 1), step), length)


def odd_tiles(width):
    return width if (width // 8) % 2 else width + 8


def cos_sin(rows, cols, length):
    angles = 2.0 * np.pi / length * ((rows[:, None] * cols[None, :]) % length)
    factor = 1.0 / math.sqrt(length)
    return np.cos(angles) * factor, np.sin(angles) * factor


def signed_of(width):
    return np.arange(width) - width // 2


def z_tables(count, length, planes, width):
    devices = length // planes
    cos, sin = cos_sin(signed_of(width), np.arange(length), length)
    cos = cos.reshape(width, devices, planes)
    sin = sin.reshape(width, devices, planes)
    table = np.zeros((2, count, width, devices, 2, count, planes), np.float32)
    for k in range(count):
        table[0, k, :, :, 0, k] = cos
        table[1, k, :, :, 0, k] = -sin
        table[0, k, :, :, 1, k] = sin
        table[1, k, :, :, 1, k] = cos
    size = count * 2
    return table.reshape(size * width, devices * size * planes)


def peers_of(axis):
    size = lax.axis_size(axis)
    me = lax.axis_index(axis)
    offs = sorted(range(1, size), key=lambda off: abs(2 * off - size))
    return me, [lax.rem(me + off, size) for off in offs]


def greet(axes):
    barrier = pltpu.get_barrier_semaphore()
    waits = 0
    for axis in axes:
        for peer in peers_of(axis)[1]:
            pl.semaphore_signal(barrier, inc=1, device_id={axis: peer}, device_id_type=MESH)
            waits += 1
    pl.semaphore_wait(barrier, waits)


def send_to(axis, peer, src, dst, send_sem, recv_sem):
    copy = pltpu.make_async_remote_copy(
        src_ref=src,
        dst_ref=dst,
        send_sem=send_sem,
        recv_sem=recv_sem,
        device_id={axis: peer},
        device_id_type=MESH,
    )
    copy.start()
    return copy


def arrived(axis, peer, dst, send_sem, recv_sem):
    pltpu.make_async_remote_copy(
        src_ref=dst,
        dst_ref=dst,
        send_sem=send_sem,
        recv_sem=recv_sem,
        device_id={axis: peer},
        device_id_type=MESH,
    ).wait_recv()


def packed(rows):
    pieces = 16 // rows.shape[0]
    lanes = rows.shape[1] // pieces
    return jnp.concatenate(
        [rows[:, p * lanes : (p + 1) * lanes] for p in range(pieces)], axis=0
    ).astype(BF16)


def unpacked(tile, rows):
    tile = tile.astype(F32)
    return jnp.concatenate(
        [tile[p * rows : (p + 1) * rows] for p in range(tile.shape[0] // rows)], axis=1
    )


def half_rows(panel_ref, half, start):
    bands = panel_ref.shape[0] // 2
    pairs = [panel_ref[half * bands + k, :, pl.ds(start, BLOCK)] for k in range(bands)]
    return jnp.concatenate(
        [pair[0:1] for pair in pairs] + [pair[1:2] for pair in pairs], axis=0
    )


def all_rows(panel_ref, start):
    return jnp.concatenate([half_rows(panel_ref, half, start) for half in range(2)], axis=0)


def signed_index(index, length):
    return jnp.where(index < length // 2, index, index - length)


def add_products(acc, slab_in, step, rows_of):
    tiles = BLOCK // 128
    deep = 2 * tiles
    rights = []
    for u in range(2):
        right = jnp.concatenate(rows_of(2 * step + u), axis=0).astype(BF16)
        rights.append(
            jnp.concatenate([right[:, t * 128 : (t + 1) * 128] for t in range(tiles)], axis=0)
        )
    right = jnp.concatenate(rights, axis=1)
    some = 32
    first = pl.multiple_of(2 * step * deep, 2 * deep)
    for j in range(0, slab_in.shape[0], some):
        left = jnp.concatenate(
            [
                slab_in[pl.ds(j, some), pl.ds(first + u * deep, deep), :].reshape(some * deep, 128)
                for u in range(2)
            ],
            axis=1,
        )
        got = lax.dot_general(left, right, NT, preferred_element_type=F32)
        for tile in range(acc.shape[0]):
            acc[tile, pl.ds(j * deep, some * deep), :] += got[:, tile * 128 : (tile + 1) * 128]


def collapse(acc, part, width):
    tiles = BLOCK // 128
    deep = 2 * tiles
    rows = acc.shape[1] // deep
    total = None
    for t in range(tiles):
        lane = t * width
        piece = acc[lane // 128, pl.ds(2 * t + part, rows, stride=deep), :]
        piece = piece[:, lane % 128 : lane % 128 + width]
        total = piece if total is None else total + piece
    return total


def one_hot(size, places):
    grid = lax.broadcasted_iota(jnp.int32, (size, places.shape[1]), 0)
    return (grid == places).astype(F32).astype(BF16)


def first_kernel(
    sizes, wide, width, slot_ref, panel_ref, columns_ref, table_ref, slab_ref,
    out_ref, pos_ref, margin_ref,
    acc, picks, thirds, stage, land, pos_mine, pos_land, coef_land, slab_in, acc_m,
    slab_sem, send_x, recv_x, send_c, recv_c, send_b, recv_b,
):
    n_one, n_two, length = sizes
    me, others = peers_of("pw")
    here, mates = peers_of("band")
    steps = slot_ref.shape[1] // BLOCK
    cols = acc.shape[1]
    side = land.shape[3] // 2
    size = 2 * panel_ref.shape[0]
    fetch = pltpu.make_async_copy(slab_ref, slab_in, slab_sem)
    fetch.start()
    greet(("pw", "band"))

    def pack(step, carry):
        start = pl.multiple_of(step * BLOCK, BLOCK)
        coef_land[here, step] = packed(all_rows(panel_ref, start))
        return carry

    lax.fori_loop(0, steps, pack, 0)
    column = columns_ref[...]
    place_one = signed_index(column // n_two, n_one) + wide // 2
    place_two = signed_index(lax.rem(column, n_two), n_two) + wide // 2
    pos_mine[...] = place_two * wide + place_one
    pos_land[me] = pos_mine[...]
    copies = []
    for peer in others:
        copies.append(
            send_to("pw", peer, pos_mine, pos_land.at[me], send_c.at[peer], recv_c.at[me])
        )
    for mate in mates:
        copies.append(
            send_to(
                "band", mate, coef_land.at[here], coef_land.at[here], send_b.at[mate],
                recv_b.at[here],
            )
        )

    for half in range(2):
        acc[...] = jnp.zeros_like(acc)

        def scatter(step, carry):
            start = pl.multiple_of(step * BLOCK, BLOCK)
            if half == 0:
                slot = slot_ref[:, pl.ds(start, BLOCK)]
                third = lax.rem(lax.rem(slot, length) + width // 2, length)
                pick_col = one_hot(cols, slot // length)
                pick_third = one_hot(width, third)
                picks[step] = pick_col
                thirds[step] = pick_third
            else:
                pick_col = picks[step]
                pick_third = thirds[step]
            values = half_rows(panel_ref, half, start).astype(BF16)
            spread = jnp.concatenate(
                [pick_third * values[q : q + 1] for q in range(values.shape[0])], axis=0
            )
            acc[...] += lax.dot_general(spread, pick_col, NT, preferred_element_type=F32)
            return carry

        lax.fori_loop(0, steps, scatter, 0)
        got = acc[...].astype(BF16)
        done = lax.dot_general(got, table_ref[...], TN, preferred_element_type=F32)
        for d in range(land.shape[0]):
            piece = done[:, d * side : (d + 1) * side]
            stage[half, d] = jnp.concatenate(
                [piece[: cols // 2], piece[cols // 2 :]], axis=1
            ).astype(BF16)
        for peer in others:
            copies.append(
                send_to(
                    "pw", peer, stage.at[half, peer], land.at[me, half],
                    send_x.at[peer, half], recv_x.at[me, half],
                )
            )
        land[me, half] = stage[half, me]

    for mate in mates:
        arrived("band", mate, coef_land.at[mate], send_b.at[mate], recv_b.at[mate])
    fetch.wait()
    acc_m[...] = jnp.zeros_like(acc_m)

    def margin(step, carry):
        add_products(
            acc_m,
            slab_in,
            step,
            lambda block: [unpacked(coef_land[b, block], size) for b in range(len(mates) + 1)],
        )
        return carry

    lax.fori_loop(0, steps // 2, margin, 0)
    for which in range(2):
        margin_ref[which] = collapse(acc_m, which, margin_ref.shape[2])
    for peer in others:
        arrived("pw", peer, pos_land.at[peer], send_c.at[peer], recv_c.at[peer])
    pos_ref[...] = pos_land[...]
    for half in range(2):
        for peer in others:
            arrived(
                "pw", peer, land.at[peer, half], send_x.at[peer, half], recv_x.at[peer, half]
            )
    out_ref[...] = land[...]
    for copy in copies:
        copy.wait_send()


def first_part(slot, panel, columns, table, slab, sizes, wide, width, devices, mates):
    count, _, n = panel.shape
    cols = columns.shape[1]
    lanes = 2 * (table.shape[1] // devices)
    steps = n // BLOCK
    rows = slab.shape[0]
    pair = 2 * count * mates
    whole = pl.BlockSpec(memory_space=pltpu.VMEM)
    anywhere = pl.BlockSpec(memory_space=pl.ANY)
    coef_shape = (mates, steps, 16, BLOCK * count // 8)
    wave_shape = (devices, 2, cols // 2, lanes)
    dma = pltpu.SemaphoreType.DMA
    return pl.pallas_call(
        functools.partial(first_kernel, sizes, wide, width),
        in_specs=[whole] * 4 + [anywhere],
        out_specs=[whole] * 3,
        out_shape=[
            jax.ShapeDtypeStruct(wave_shape, BF16),
            jax.ShapeDtypeStruct((devices, 1, cols), jnp.int32),
            jax.ShapeDtypeStruct((2, rows, pair), F32),
        ],
        scratch_shapes=[
            pltpu.VMEM((count * width, cols), F32),
            pltpu.VMEM((steps, cols, BLOCK), BF16),
            pltpu.VMEM((steps, width, BLOCK), BF16),
            pltpu.VMEM((2, devices, cols // 2, lanes), BF16),
            pltpu.VMEM(wave_shape, BF16),
            pltpu.VMEM((1, cols), jnp.int32),
            pltpu.VMEM((devices, 1, cols), jnp.int32),
            pltpu.VMEM(coef_shape, BF16),
            pltpu.VMEM(slab.shape, BF16),
            pltpu.VMEM((pair * BLOCK // 128 // 128, rows * BLOCK // 64, 128), F32),
            dma,
            dma((devices, 2)),
            dma((devices, 2)),
            dma((devices,)),
            dma((devices,)),
            dma((mates,)),
            dma((mates,)),
        ],
        compiler_params=pltpu.CompilerParams(
            vmem_limit_bytes=LIMIT, collective_id=1, has_side_effects=True
        ),
        name="first_part",
    )(slot, panel, columns, table, slab)


def plane_kernel(
    wide, n_one, n_two, pos_ref, x_ref, tx_ref, ty_ref, tyb_ref, txb_ref, v_ref, out_ref,
    wave, box, mid, mid_back,
):
    total, lanes = wave.shape
    planes = v_ref.shape[0] // n_one
    sign = jnp.where(
        lax.broadcasted_iota(jnp.int32, (1, lanes), 1) < lanes // 2, -1.0, 1.0
    ).astype(F32)
    devices, _, rows, _ = x_ref.shape
    piece = lanes // 4

    def quarters(tile):
        return [tile[:, p * piece : (p + 1) * piece] for p in range(4)]

    def unfold(d, carry):
        low = quarters(x_ref[d, 0].astype(F32))
        high = quarters(x_ref[d, 1].astype(F32))
        for side in range(2):
            base = pl.multiple_of((2 * d + side) * rows, rows)
            wave[pl.ds(base, rows), :] = jnp.concatenate(
                [low[2 * side], high[2 * side], low[2 * side + 1], high[2 * side + 1]], axis=1
            )
        return carry

    lax.fori_loop(0, devices, unfold, 0)
    box[...] = jnp.zeros_like(box)
    group = 16

    def put(step, carry):
        base = pl.multiple_of(step * group, group)
        tile = wave[pl.ds(base, group), :]
        for u in range(group):
            box[pl.ds(pos_ref[base + u], 1), :] = tile[u : u + 1]
        return carry

    lax.fori_loop(0, total // group, put, 0)

    def stacked(tiles):
        plain = jnp.concatenate(tiles, axis=1)
        turned = jnp.concatenate(
            [pltpu.roll(tile, lanes // 2, 1) * sign for tile in tiles], axis=1
        )
        return jnp.concatenate([plain, turned], axis=0).astype(BF16)

    def split(got):
        return [got[:, u * lanes : (u + 1) * lanes] for u in range(got.shape[1] // lanes)]

    def inverse_one(step, carry):
        tiles = [box[pl.ds(pl.multiple_of((2 * step + u) * wide, 8), wide), :] for u in range(2)]
        got = jnp.dot(tx_ref[...], stacked(tiles), preferred_element_type=F32)
        for u, tile in enumerate(split(got)):
            mid[pl.ds(2 * step + u, n_one, stride=wide), :] = tile
        return carry

    lax.fori_loop(0, wide // 2, inverse_one, 0, unroll=4)

    def both_two(step, carry):
        starts = [pl.multiple_of((2 * step + u) * wide, 8) for u in range(2)]
        tiles = [mid[pl.ds(start, wide), :] for start in starts]
        got = jnp.dot(ty_ref[...], stacked(tiles), preferred_element_type=F32)
        tiles = []
        for u, tile in enumerate(split(got)):
            local = v_ref[pl.ds(2 * step + u, planes, stride=n_one), :]
            tiles.append(tile * jnp.concatenate([local] * (lanes // planes), axis=0).T)
        back = jnp.dot(tyb_ref[...], stacked(tiles), preferred_element_type=F32)
        for u, tile in enumerate(split(back)):
            mid_back[pl.ds(starts[u], wide), :] = tile
        return carry

    lax.fori_loop(0, n_one // 2, both_two, 0, unroll=4)

    def forward_one(step, carry):
        tiles = [mid_back[pl.ds(2 * step + u, n_one, stride=wide), :] for u in range(2)]
        got = jnp.dot(txb_ref[...], stacked(tiles), preferred_element_type=F32)
        for u, tile in enumerate(split(got)):
            start = pl.multiple_of((2 * step + u) * wide, 8)
            box[pl.ds(start, wide), :] = tile
        return carry

    lax.fori_loop(0, wide // 2, forward_one, 0, unroll=4)

    def take(step, carry):
        base = pl.multiple_of(step * group, group)
        taken = [box[pl.ds(pos_ref[base + u], 1), :] for u in range(group)]
        for u in range(group):
            wave[pl.ds(base + u, 1), :] = taken[u]
        return carry

    lax.fori_loop(0, total // group, take, 0)

    def fold(d, carry):
        sides = [
            quarters(wave[pl.ds(pl.multiple_of((2 * d + side) * rows, rows), rows), :])
            for side in range(2)
        ]
        for half in range(2):
            out_ref[d, half] = jnp.concatenate(
                [sides[side][half + 2 * which] for side in range(2) for which in range(2)], axis=1
            ).astype(BF16)
        return carry

    lax.fori_loop(0, devices, fold, 0)


def plane_part(pos, x, tables, potential_rows, wide, n_one, n_two):
    devices, _, rows, lanes = x.shape
    total = 2 * devices * rows
    whole = pl.BlockSpec(memory_space=pltpu.VMEM)
    return pl.pallas_call(
        functools.partial(plane_kernel, wide, n_one, n_two),
        in_specs=[pl.BlockSpec(memory_space=pltpu.SMEM)] + [whole] * 6,
        out_specs=whole,
        out_shape=jax.ShapeDtypeStruct(x.shape, BF16),
        scratch_shapes=[
            pltpu.VMEM((total, lanes), F32),
            pltpu.VMEM((wide * wide, lanes), F32),
            pltpu.VMEM((n_one * wide, lanes), F32),
            pltpu.VMEM((n_one * wide, lanes), F32),
        ],
        compiler_params=pltpu.CompilerParams(vmem_limit_bytes=LIMIT),
        name="plane_part",
    )(pos, x, *tables, potential_rows)


def last_kernel(
    sizes, width, groups, slot_ref, panel_ref, columns_ref, x_ref, table_ref, margin_ref,
    slab_ref, out_ref,
    home, held, picks, kinetics, app, slab_in, acc_h, part, parts,
    slab_sem, send_x, recv_x, send_b, recv_b, send_p, recv_p,
):
    n_one, n_two, length = sizes
    me, others = peers_of("pw")
    here, mates = peers_of("band")
    bands = len(mates) + 1
    count = panel_ref.shape[0]
    size = 2 * count
    body = count * width
    cols = held.shape[1]
    steps = slot_ref.shape[1] // BLOCK
    each = steps // groups
    fetch = pltpu.make_async_copy(slab_ref, slab_in, slab_sem)
    fetch.start()
    greet(("pw", "band"))
    copies = []
    for half in range(2):
        for peer in others:
            copies.append(
                send_to(
                    "pw", peer, x_ref.at[peer, half], home.at[me, half],
                    send_x.at[peer, half], recv_x.at[me, half],
                )
            )
    home[me] = x_ref[me]
    column = columns_ref[...]
    held[body:, :] = jnp.concatenate(
        [
            signed_index(column // n_two, n_one),
            signed_index(lax.rem(column, n_two), n_two),
            jnp.zeros((14, cols), jnp.int32),
        ],
        axis=0,
    ).astype(F32).astype(BF16)
    acc_h[...] = jnp.zeros_like(acc_h)
    fetch.wait()

    for half in range(2):
        for peer in others:
            arrived(
                "pw", peer, home.at[peer, half], send_x.at[peer, half], recv_x.at[peer, half]
            )
        pieces = [home[d, half].astype(F32) for d in range(home.shape[0])]
        side = home.shape[3] // 2
        x = jnp.concatenate(
            [
                jnp.concatenate([piece[:, :side] for piece in pieces], axis=1),
                jnp.concatenate([piece[:, side:] for piece in pieces], axis=1),
            ],
            axis=0,
        ).astype(BF16)
        held[:body, :] = lax.dot_general(
            table_ref[...], x, NT, preferred_element_type=F32
        ).astype(BF16)

        def gather(step, carry):
            start = pl.multiple_of(step * BLOCK, BLOCK)
            slot = slot_ref[:, pl.ds(start, BLOCK)]
            third = lax.rem(slot, length)
            place = lax.rem(third + width // 2, length)
            at_third = lax.broadcasted_iota(jnp.int32, (width, BLOCK), 0) == place
            if half == 0:
                pick_col = one_hot(cols, slot // length)
                picks[step] = pick_col
                got = jnp.dot(held[...], pick_col, preferred_element_type=F32)
                f_one = got[body : body + 1] * (2.0 / n_one)
                f_two = got[body + 1 : body + 2] * (2.0 / n_two)
                f_three = signed_index(third, length).astype(F32) * (2.0 / length)
                kinetic = 0.5 * (f_one * f_one + f_two * f_two + f_three * f_three)
                kinetics[:, pl.ds(start, BLOCK)] = kinetic
            else:
                got = jnp.dot(held[:body, :], picks[step], preferred_element_type=F32)
                kinetic = kinetics[:, pl.ds(start, BLOCK)]
            picked = jnp.concatenate(
                [
                    jnp.sum(
                        jnp.where(at_third, got[q * width : (q + 1) * width], 0.0),
                        axis=0,
                        keepdims=True,
                    )
                    for q in range(count)
                ],
                axis=0,
            )
            app[here, half, step] = packed(kinetic * half_rows(panel_ref, half, start) + picked)
            return carry

        for g in range(groups):
            lax.fori_loop(g * each, (g + 1) * each, gather, 0)
            span = pl.ds(g * each, each)
            for mate in mates:
                copies.append(
                    send_to(
                        "band", mate, app.at[here, half, span], app.at[here, half, span],
                        send_b.at[mate, half, g], recv_b.at[here, half, g],
                    )
                )

    def hamiltonian(step, carry):
        add_products(
            acc_h,
            slab_in,
            step,
            lambda block: [
                unpacked(app[b, half, block], count) for b in range(bands) for half in range(2)
            ],
        )
        return carry

    for g in range(groups):
        span = pl.ds(g * each, each)
        for mate in mates:
            for half in range(2):
                arrived(
                    "band", mate, app.at[mate, half, span], send_b.at[mate, half, g],
                    recv_b.at[mate, half, g],
                )
        lax.fori_loop(g * each // 2, (g + 1) * each // 2, hamiltonian, 0)

    width_h = margin_ref.shape[2]
    real_rows, imag_rows = [
        jnp.concatenate([collapse(acc_h, which, width_h), margin_ref[which]], axis=1).T
        for which in range(2)
    ]

    def pick(value, kind, which):
        first = kind * bands * size + which * (count // 2)
        return jnp.concatenate(
            [value[first + b * count : first + b * count + count // 2] for b in range(2 * bands)],
            axis=0,
        )

    pieces = []
    for kind in range(2):
        pieces.append(pick(real_rows, kind, 0) + pick(imag_rows, kind, 1))
        pieces.append(pick(real_rows, kind, 1) - pick(imag_rows, kind, 0))
    part[...] = jnp.concatenate(pieces, axis=0)
    share = out_ref.shape[0]

    def block_of(index):
        return pl.ds(pl.multiple_of(index * share, share), share)

    for peer in others:
        copies.append(
            send_to(
                "pw", peer, part.at[block_of(peer)], parts.at[me], send_p.at[peer], recv_p.at[me]
            )
        )
    parts[me] = part[block_of(me), :]
    for peer in others:
        arrived("pw", peer, parts.at[peer], send_p.at[peer], recv_p.at[peer])
    total = parts[0]
    for d in range(1, parts.shape[0]):
        total = total + parts[d]
    out_ref[...] = total
    for copy in copies:
        copy.wait_send()


def last_part(slot, panel, columns, x, table, margin, slab, sizes, width, mates):
    devices = x.shape[0]
    cols = columns.shape[1]
    count, _, n = panel.shape
    steps = n // BLOCK
    size = 2 * count
    rows = slab.shape[0]
    groups = 3 if steps % 6 == 0 else 1
    share = 2 * mates * size // devices
    whole = pl.BlockSpec(memory_space=pltpu.VMEM)
    anywhere = pl.BlockSpec(memory_space=pl.ANY)
    dma = pltpu.SemaphoreType.DMA
    return pl.pallas_call(
        functools.partial(last_kernel, sizes, width, groups),
        in_specs=[whole] * 6 + [anywhere],
        out_specs=whole,
        out_shape=jax.ShapeDtypeStruct((share, rows), F32),
        scratch_shapes=[
            pltpu.VMEM(x.shape, BF16),
            pltpu.VMEM((count * width + 16, cols), BF16),
            pltpu.VMEM((steps, cols, BLOCK), BF16),
            pltpu.VMEM((1, n), F32),
            pltpu.VMEM((mates, 2, steps, 16, BLOCK * count // 16), BF16),
            pltpu.VMEM(slab.shape, BF16),
            pltpu.VMEM((mates * size * BLOCK // 128 // 128, rows * BLOCK // 64, 128), F32),
            pltpu.VMEM((2 * mates * size, rows), F32),
            pltpu.VMEM((devices, share, rows), F32),
            dma,
            dma((devices, 2)),
            dma((devices, 2)),
            dma((mates, 2, groups)),
            dma((mates, 2, groups)),
            dma((devices,)),
            dma((devices,)),
        ],
        compiler_params=pltpu.CompilerParams(
            vmem_limit_bytes=LIMIT, collective_id=2, has_side_effects=True
        ),
        name="last_part",
    )(slot, panel, columns, x, table, margin, slab)


def per_device(slab, panel, potential, pw_slot, columns):
    devices = lax.axis_size("pw")
    mates = lax.axis_size("band")
    planes, n_one, n_two = potential.shape
    length = planes * devices
    cols = columns.shape[0]
    count = panel.shape[0]
    n = panel.shape[2]

    square = disk_square(n_one, n_two, cols * devices)
    wide = odd_tiles(window(math.isqrt(square), 8, max(n_one, n_two)))
    reach = math.isqrt(square + (-(-n // (2 * cols)) + 2) ** 2) + 1
    width = window(reach, 16, length)

    ztab = jnp.asarray(z_tables(count // 2, length, planes, width), BF16)
    cy, sy = cos_sin(np.arange(n_two), signed_of(wide), n_two)
    cx, sx = cos_sin(np.arange(n_one), signed_of(wide), n_one)
    tables = [
        np.concatenate([cx, sx], axis=1),
        np.concatenate([cy, sy], axis=1),
        np.concatenate([cy.T, -sy.T], axis=1),
        np.concatenate([cx.T, -sx.T], axis=1),
    ]
    tables = [jnp.asarray(t, BF16) for t in tables]

    slot = pw_slot.reshape(1, n)
    owned = columns.reshape(1, cols)
    sizes = (n_one, n_two, length)
    slab = slab.reshape(slab.shape[0], 2, n // 128, 128)
    slab = slab.transpose(0, 2, 1, 3).reshape(slab.shape[0], n // 64, 128)
    there, pos, margin = first_part(
        slot, panel, owned, ztab, slab, sizes, wide, width, devices, mates
    )
    worked = plane_part(
        pos.reshape(devices * cols), there, tables, potential.reshape(planes * n_one, n_two), wide, n_one, n_two
    )
    out = last_part(
        slot, panel, owned, worked, ztab, margin, slab, sizes, width, mates
    )
    return out.T


def solution(mesh):
    in_specs = (P("band", None, "pw"), P("band", None, "pw"), P("pw", None, None), P("pw"), P("pw"))
    out_specs = P("band", "pw")
    return jax.shard_map(
        per_device, mesh=mesh, in_specs=in_specs, out_specs=out_specs, check_vma=False
    )
```

```python
import functools
import math

import jax
import jax.numpy as jnp
import numpy as np
from jax import lax
from jax.experimental import pallas as pl
from jax.experimental.pallas import tpu as pltpu
from jax.sharding import PartitionSpec as P

F32 = jnp.float32
BF16 = jnp.bfloat16
NT = (((1,), (1,)), ((), ()))
TN = (((0,), (0,)), ((), ()))
MESH = pl.DeviceIdType.MESH
BLOCK = 1024
LIMIT = 56 * 1024 * 1024


def round_up(value, step):
    return -(-value // step) * step


def disk_square(first_len, second_len, count):
    one = np.arange(first_len) - first_len // 2
    two = np.arange(second_len) - second_len // 2
    return int(np.sort((one[:, None] ** 2 + two[None, :] ** 2).ravel())[count - 1])


def window(half, step, length):
    return min(round_up(2 * (half + 1), step), length)


def odd_tiles(width):
    return width if (width // 8) % 2 else width + 8


def cos_sin(rows, cols, length):
    angles = 2.0 * np.pi / length * ((rows[:, None] * cols[None, :]) % length)
    factor = 1.0 / math.sqrt(length)
    return np.cos(angles) * factor, np.sin(angles) * factor


def signed_of(width):
    return np.arange(width) - width // 2


def z_tables(count, length, planes, width):
    devices = length // planes
    cos, sin = cos_sin(signed_of(width), np.arange(length), length)
    cos = cos.reshape(width, devices, planes)
    sin = sin.reshape(width, devices, planes)
    table = np.zeros((2, count, width, devices, 2, count, planes), np.float32)
    for k in range(count):
        table[0, k, :, :, 0, k] = cos
        table[1, k, :, :, 0, k] = -sin
        table[0, k, :, :, 1, k] = sin
        table[1, k, :, :, 1, k] = cos
    size = count * 2
    return table.reshape(size * width, devices * size * planes)


def peers_of(axis):
    size = lax.axis_size(axis)
    me = lax.axis_index(axis)
    offs = sorted(range(1, size), key=lambda off: abs(2 * off - size))
    return me, [lax.rem(me + off, size) for off in offs]


def greet(axes):
    barrier = pltpu.get_barrier_semaphore()
    waits = 0
    for axis in axes:
        for peer in peers_of(axis)[1]:
            pl.semaphore_signal(barrier, inc=1, device_id={axis: peer}, device_id_type=MESH)
            waits += 1
    pl.semaphore_wait(barrier, waits)


def send_to(axis, peer, src, dst, send_sem, recv_sem):
    copy = pltpu.make_async_remote_copy(
        src_ref=src,
        dst_ref=dst,
        send_sem=send_sem,
        recv_sem=recv_sem,
        device_id={axis: peer},
        device_id_type=MESH,
    )
    copy.start()
    return copy


def arrived(axis, peer, dst, send_sem, recv_sem):
    pltpu.make_async_remote_copy(
        src_ref=dst,
        dst_ref=dst,
        send_sem=send_sem,
        recv_sem=recv_sem,
        device_id={axis: peer},
        device_id_type=MESH,
    ).wait_recv()


def packed(rows):
    pieces = 16 // rows.shape[0]
    lanes = rows.shape[1] // pieces
    return jnp.concatenate(
        [rows[:, p * lanes : (p + 1) * lanes] for p in range(pieces)], axis=0
    ).astype(BF16)


def unpacked(tile, rows):
    tile = tile.astype(F32)
    return jnp.concatenate(
        [tile[p * rows : (p + 1) * rows] for p in range(tile.shape[0] // rows)], axis=1
    )


def half_rows(panel_ref, half, start):
    bands = panel_ref.shape[0] // 2
    pairs = [panel_ref[half * bands + k, :, pl.ds(start, BLOCK)] for k in range(bands)]
    return jnp.concatenate(
        [pair[0:1] for pair in pairs] + [pair[1:2] for pair in pairs], axis=0
    )


def all_rows(panel_ref, start):
    return jnp.concatenate([half_rows(panel_ref, half, start) for half in range(2)], axis=0)


def signed_index(index, length):
    return jnp.where(index < length // 2, index, index - length)


def add_products(acc, slab_in, step, rows_of):
    tiles = BLOCK // 128
    deep = 2 * tiles
    rights = []
    for u in range(2):
        right = jnp.concatenate(rows_of(2 * step + u), axis=0).astype(BF16)
        rights.append(
            jnp.concatenate([right[:, t * 128 : (t + 1) * 128] for t in range(tiles)], axis=0)
        )
    right = jnp.concatenate(rights, axis=1)
    some = 32
    first = pl.multiple_of(2 * step * deep, 2 * deep)
    for j in range(0, slab_in.shape[0], some):
        left = jnp.concatenate(
            [
                slab_in[pl.ds(j, some), pl.ds(first + u * deep, deep), :].reshape(some * deep, 128)
                for u in range(2)
            ],
            axis=1,
        )
        got = lax.dot_general(left, right, NT, preferred_element_type=F32)
        for tile in range(acc.shape[0]):
            acc[tile, pl.ds(j * deep, some * deep), :] += got[:, tile * 128 : (tile + 1) * 128]


def collapse(acc, part, width):
    tiles = BLOCK // 128
    deep = 2 * tiles
    rows = acc.shape[1] // deep
    total = None
    for t in range(tiles):
        lane = t * width
        piece = acc[lane // 128, pl.ds(2 * t + part, rows, stride=deep), :]
        piece = piece[:, lane % 128 : lane % 128 + width]
        total = piece if total is None else total + piece
    return total


def one_hot(size, places):
    grid = lax.broadcasted_iota(jnp.int32, (size, places.shape[1]), 0)
    return (grid == places).astype(F32).astype(BF16)


def first_kernel(
    sizes, wide, width, slot_ref, panel_ref, columns_ref, table_ref, slab_ref,
    out_ref, pos_ref, margin_ref,
    acc, picks, thirds, stage, land, pos_mine, pos_land, coef_land, slab_in, acc_m,
    slab_sem, send_x, recv_x, send_c, recv_c, send_b, recv_b,
):
    n_one, n_two, length = sizes
    me, others = peers_of("pw")
    here, mates = peers_of("band")
    steps = slot_ref.shape[1] // BLOCK
    cols = acc.shape[1]
    side = land.shape[3] // 2
    size = 2 * panel_ref.shape[0]
    fetch = pltpu.make_async_copy(slab_ref, slab_in, slab_sem)
    fetch.start()
    greet(("pw", "band"))

    def pack(step, carry):
        start = pl.multiple_of(step * BLOCK, BLOCK)
        coef_land[here, step] = packed(all_rows(panel_ref, start))
        return carry

    lax.fori_loop(0, steps, pack, 0)
    column = columns_ref[...]
    place_one = signed_index(column // n_two, n_one) + wide // 2
    place_two = signed_index(lax.rem(column, n_two), n_two) + wide // 2
    pos_mine[...] = place_two * wide + place_one
    pos_land[me] = pos_mine[...]
    copies = []
    for peer in others:
        copies.append(
            send_to("pw", peer, pos_mine, pos_land.at[me], send_c.at[peer], recv_c.at[me])
        )
    for mate in mates:
        copies.append(
            send_to(
                "band", mate, coef_land.at[here], coef_land.at[here], send_b.at[mate],
                recv_b.at[here],
            )
        )

    for half in range(2):
        acc[...] = jnp.zeros_like(acc)

        def scatter(step, carry):
            start = pl.multiple_of(step * BLOCK, BLOCK)
            if half == 0:
                slot = slot_ref[:, pl.ds(start, BLOCK)]
                third = lax.rem(lax.rem(slot, length) + width // 2, length)
                down = jnp.broadcast_to(slot // length, (8, BLOCK)).T[:, 0:1]
                across = lax.broadcasted_iota(jnp.int32, (BLOCK, cols), 1)
                pick_col = (across == down).astype(F32).astype(BF16)
                pick_third = one_hot(width, third)
                picks[step] = pick_col
                thirds[step] = pick_third
            else:
                pick_col = picks[step]
                pick_third = thirds[step]
            values = half_rows(panel_ref, half, start).astype(BF16)
            spread = jnp.concatenate(
                [pick_third * values[q : q + 1] for q in range(values.shape[0])], axis=0
            )
            acc[...] += jnp.dot(spread, pick_col, preferred_element_type=F32)
            return carry

        lax.fori_loop(0, steps, scatter, 0)
        got = acc[...].astype(BF16)
        done = lax.dot_general(got, table_ref[...], TN, preferred_element_type=F32)
        for d in range(land.shape[0]):
            piece = done[:, d * side : (d + 1) * side]
            stage[half, d] = jnp.concatenate(
                [piece[: cols // 2], piece[cols // 2 :]], axis=1
            ).astype(BF16)
        for peer in others:
            copies.append(
                send_to(
                    "pw", peer, stage.at[half, peer], land.at[me, half],
                    send_x.at[peer, half], recv_x.at[me, half],
                )
            )
        land[me, half] = stage[half, me]

    for mate in mates:
        arrived("band", mate, coef_land.at[mate], send_b.at[mate], recv_b.at[mate])
    fetch.wait()
    acc_m[...] = jnp.zeros_like(acc_m)

    def margin(step, carry):
        add_products(
            acc_m,
            slab_in,
            step,
            lambda block: [unpacked(coef_land[b, block], size) for b in range(len(mates) + 1)],
        )
        return carry

    lax.fori_loop(0, steps // 2, margin, 0)
    for which in range(2):
        margin_ref[which] = collapse(acc_m, which, margin_ref.shape[2])
    for peer in others:
        arrived("pw", peer, pos_land.at[peer], send_c.at[peer], recv_c.at[peer])
    pos_ref[...] = pos_land[...]
    for half in range(2):
        for peer in others:
            arrived(
                "pw", peer, land.at[peer, half], send_x.at[peer, half], recv_x.at[peer, half]
            )
    out_ref[...] = land[...]
    for copy in copies:
        copy.wait_send()


def first_part(slot, panel, columns, table, slab, sizes, wide, width, devices, mates):
    count, _, n = panel.shape
    cols = columns.shape[1]
    lanes = 2 * (table.shape[1] // devices)
    steps = n // BLOCK
    rows = slab.shape[0]
    pair = 2 * count * mates
    whole = pl.BlockSpec(memory_space=pltpu.VMEM)
    anywhere = pl.BlockSpec(memory_space=pl.ANY)
    coef_shape = (mates, steps, 16, BLOCK * count // 8)
    wave_shape = (devices, 2, cols // 2, lanes)
    dma = pltpu.SemaphoreType.DMA
    return pl.pallas_call(
        functools.partial(first_kernel, sizes, wide, width),
        in_specs=[whole] * 4 + [anywhere],
        out_specs=[whole] * 3,
        out_shape=[
            jax.ShapeDtypeStruct(wave_shape, BF16),
            jax.ShapeDtypeStruct((devices, 1, cols), jnp.int32),
            jax.ShapeDtypeStruct((2, rows, pair), F32),
        ],
        scratch_shapes=[
            pltpu.VMEM((count * width, cols), F32),
            pltpu.VMEM((steps, BLOCK, cols), BF16),
            pltpu.VMEM((steps, width, BLOCK), BF16),
            pltpu.VMEM((2, devices, cols // 2, lanes), BF16),
            pltpu.VMEM(wave_shape, BF16),
            pltpu.VMEM((1, cols), jnp.int32),
            pltpu.VMEM((devices, 1, cols), jnp.int32),
            pltpu.VMEM(coef_shape, BF16),
            pltpu.VMEM(slab.shape, BF16),
            pltpu.VMEM((pair * BLOCK // 128 // 128, rows * BLOCK // 64, 128), F32),
            dma,
            dma((devices, 2)),
            dma((devices, 2)),
            dma((devices,)),
            dma((devices,)),
            dma((mates,)),
            dma((mates,)),
        ],
        compiler_params=pltpu.CompilerParams(
            vmem_limit_bytes=LIMIT, collective_id=1, has_side_effects=True
        ),
        name="first_part",
    )(slot, panel, columns, table, slab)


def plane_kernel(
    wide, n_one, n_two, pos_ref, x_ref, tx_ref, ty_ref, tyb_ref, txb_ref, v_ref, out_ref,
    wave, box, mid, mid_back,
):
    total, lanes = wave.shape
    planes = v_ref.shape[0] // n_one
    sign = jnp.where(
        lax.broadcasted_iota(jnp.int32, (1, lanes), 1) < lanes // 2, -1.0, 1.0
    ).astype(F32)
    devices, _, rows, _ = x_ref.shape
    piece = lanes // 4

    def quarters(tile):
        return [tile[:, p * piece : (p + 1) * piece] for p in range(4)]

    def unfold(d, carry):
        low = quarters(x_ref[d, 0].astype(F32))
        high = quarters(x_ref[d, 1].astype(F32))
        for side in range(2):
            base = pl.multiple_of((2 * d + side) * rows, rows)
            wave[pl.ds(base, rows), :] = jnp.concatenate(
                [low[2 * side], high[2 * side], low[2 * side + 1], high[2 * side + 1]], axis=1
            )
        return carry

    lax.fori_loop(0, devices, unfold, 0)
    box[...] = jnp.zeros_like(box)
    group = 16

    def put(step, carry):
        base = pl.multiple_of(step * group, group)
        tile = wave[pl.ds(base, group), :]
        for u in range(group):
            box[pl.ds(pos_ref[base + u], 1), :] = tile[u : u + 1]
        return carry

    lax.fori_loop(0, total // group, put, 0)

    def stacked(tiles):
        plain = jnp.concatenate(tiles, axis=1)
        turned = jnp.concatenate(
            [pltpu.roll(tile, lanes // 2, 1) * sign for tile in tiles], axis=1
        )
        return jnp.concatenate([plain, turned], axis=0).astype(BF16)

    def split(got):
        return [got[:, u * lanes : (u + 1) * lanes] for u in range(got.shape[1] // lanes)]

    def inverse_one(step, carry):
        tiles = [box[pl.ds(pl.multiple_of((2 * step + u) * wide, 8), wide), :] for u in range(2)]
        got = jnp.dot(tx_ref[...], stacked(tiles), preferred_element_type=F32)
        for u, tile in enumerate(split(got)):
            mid[pl.ds(2 * step + u, n_one, stride=wide), :] = tile
        return carry

    lax.fori_loop(0, wide // 2, inverse_one, 0, unroll=4)

    def both_two(step, carry):
        starts = [pl.multiple_of((2 * step + u) * wide, 8) for u in range(2)]
        tiles = [mid[pl.ds(start, wide), :] for start in starts]
        got = jnp.dot(ty_ref[...], stacked(tiles), preferred_element_type=F32)
        local = jnp.concatenate(
            [
                jnp.concatenate(
                    [v_ref[pl.ds(2 * step + u, planes, stride=n_one), :]] * (lanes // planes),
                    axis=0,
                ).T
                for u in range(2)
            ],
            axis=1,
        )
        both = (got * jnp.concatenate([local, local], axis=0)).astype(BF16)
        back = jnp.dot(tyb_ref[...], both, preferred_element_type=F32)
        for u, tile in enumerate(split(back)):
            mid_back[pl.ds(starts[u], wide), :] = tile
        return carry

    lax.fori_loop(0, n_one // 2, both_two, 0, unroll=4)

    def forward_one(step, carry):
        tiles = [mid_back[pl.ds(2 * step + u, n_one, stride=wide), :] for u in range(2)]
        got = jnp.dot(txb_ref[...], stacked(tiles), preferred_element_type=F32)
        for u, tile in enumerate(split(got)):
            start = pl.multiple_of((2 * step + u) * wide, 8)
            box[pl.ds(start, wide), :] = tile
        return carry

    lax.fori_loop(0, wide // 2, forward_one, 0, unroll=4)

    def take(step, carry):
        base = pl.multiple_of(step * group, group)
        taken = [box[pl.ds(pos_ref[base + u], 1), :] for u in range(group)]
        for u in range(group):
            wave[pl.ds(base + u, 1), :] = taken[u]
        return carry

    lax.fori_loop(0, total // group, take, 0)

    def fold(d, carry):
        sides = [
            quarters(wave[pl.ds(pl.multiple_of((2 * d + side) * rows, rows), rows), :])
            for side in range(2)
        ]
        for half in range(2):
            out_ref[d, half] = jnp.concatenate(
                [sides[side][half + 2 * which] for side in range(2) for which in range(2)], axis=1
            ).astype(BF16)
        return carry

    lax.fori_loop(0, devices, fold, 0)


def plane_part(pos, x, tables, potential_rows, wide, n_one, n_two):
    devices, _, rows, lanes = x.shape
    total = 2 * devices * rows
    whole = pl.BlockSpec(memory_space=pltpu.VMEM)
    return pl.pallas_call(
        functools.partial(plane_kernel, wide, n_one, n_two),
        in_specs=[pl.BlockSpec(memory_space=pltpu.SMEM)] + [whole] * 6,
        out_specs=whole,
        out_shape=jax.ShapeDtypeStruct(x.shape, BF16),
        scratch_shapes=[
            pltpu.VMEM((total, lanes), F32),
            pltpu.VMEM((wide * wide, lanes), F32),
            pltpu.VMEM((n_one * wide, lanes), F32),
            pltpu.VMEM((n_one * wide, lanes), F32),
        ],
        compiler_params=pltpu.CompilerParams(vmem_limit_bytes=LIMIT),
        name="plane_part",
    )(pos, x, *tables, potential_rows)


def last_kernel(
    sizes, width, groups, slot_ref, panel_ref, columns_ref, x_ref, table_ref, margin_ref,
    slab_ref, out_ref,
    home, held, picks, kinetics, app, slab_in, acc_h, part, parts,
    slab_sem, send_x, recv_x, send_b, recv_b, send_p, recv_p,
):
    n_one, n_two, length = sizes
    me, others = peers_of("pw")
    here, mates = peers_of("band")
    bands = len(mates) + 1
    count = panel_ref.shape[0]
    size = 2 * count
    body = count * width
    cols = held.shape[1]
    steps = slot_ref.shape[1] // BLOCK
    each = steps // groups
    fetch = pltpu.make_async_copy(slab_ref, slab_in, slab_sem)
    fetch.start()
    greet(("pw", "band"))
    copies = []
    for half in range(2):
        for peer in others:
            copies.append(
                send_to(
                    "pw", peer, x_ref.at[peer, half], home.at[me, half],
                    send_x.at[peer, half], recv_x.at[me, half],
                )
            )
    home[me] = x_ref[me]
    column = columns_ref[...]
    held[body:, :] = jnp.concatenate(
        [
            signed_index(column // n_two, n_one),
            signed_index(lax.rem(column, n_two), n_two),
            jnp.zeros((14, cols), jnp.int32),
        ],
        axis=0,
    ).astype(F32).astype(BF16)
    acc_h[...] = jnp.zeros_like(acc_h)
    fetch.wait()

    for half in range(2):
        for peer in others:
            arrived(
                "pw", peer, home.at[peer, half], send_x.at[peer, half], recv_x.at[peer, half]
            )
        pieces = [home[d, half].astype(F32) for d in range(home.shape[0])]
        side = home.shape[3] // 2
        x = jnp.concatenate(
            [
                jnp.concatenate([piece[:, :side] for piece in pieces], axis=1),
                jnp.concatenate([piece[:, side:] for piece in pieces], axis=1),
            ],
            axis=0,
        ).astype(BF16)
        held[:body, :] = lax.dot_general(
            table_ref[...], x, NT, preferred_element_type=F32
        ).astype(BF16)

        def gather(step, carry):
            start = pl.multiple_of(step * BLOCK, BLOCK)
            slot = slot_ref[:, pl.ds(start, BLOCK)]
            third = lax.rem(slot, length)
            place = lax.rem(third + width // 2, length)
            at_third = lax.broadcasted_iota(jnp.int32, (width, BLOCK), 0) == place
            if half == 0:
                pick_col = one_hot(cols, slot // length)
                picks[step] = pick_col
                got = jnp.dot(held[...], pick_col, preferred_element_type=F32)
                f_one = got[body : body + 1] * (2.0 / n_one)
                f_two = got[body + 1 : body + 2] * (2.0 / n_two)
                f_three = signed_index(third, length).astype(F32) * (2.0 / length)
                kinetic = 0.5 * (f_one * f_one + f_two * f_two + f_three * f_three)
                kinetics[:, pl.ds(start, BLOCK)] = kinetic
            else:
                got = jnp.dot(held[:body, :], picks[step], preferred_element_type=F32)
                kinetic = kinetics[:, pl.ds(start, BLOCK)]
            picked = jnp.concatenate(
                [
                    jnp.sum(
                        jnp.where(at_third, got[q * width : (q + 1) * width], 0.0),
                        axis=0,
                        keepdims=True,
                    )
                    for q in range(count)
                ],
                axis=0,
            )
            app[here, half, step] = packed(kinetic * half_rows(panel_ref, half, start) + picked)
            return carry

        for g in range(groups):
            lax.fori_loop(g * each, (g + 1) * each, gather, 0)
            span = pl.ds(g * each, each)
            for mate in mates:
                copies.append(
                    send_to(
                        "band", mate, app.at[here, half, span], app.at[here, half, span],
                        send_b.at[mate, half, g], recv_b.at[here, half, g],
                    )
                )

    for half in range(2):

        def hamiltonian(step, carry):
            add_products(
                acc_h.at[half],
                slab_in,
                step,
                lambda block: [unpacked(app[b, half, block], count) for b in range(bands)],
            )
            return carry

        for g in range(groups):
            span = pl.ds(g * each, each)
            for mate in mates:
                arrived(
                    "band", mate, app.at[mate, half, span], send_b.at[mate, half, g],
                    recv_b.at[mate, half, g],
                )
            lax.fori_loop(g * each // 2, (g + 1) * each // 2, hamiltonian, 0)

    real_rows, imag_rows = [
        jnp.concatenate(
            [collapse(acc_h.at[half], which, bands * count) for half in range(2)]
            + [margin_ref[which]],
            axis=1,
        ).T
        for which in range(2)
    ]

    def pick(value, kind, which):
        firsts = [
            (half * bands + b if kind == 0 else (bands + b) * 2 + half) * count
            + which * (count // 2)
            for b in range(bands)
            for half in range(2)
        ]
        return jnp.concatenate([value[first : first + count // 2] for first in firsts], axis=0)

    pieces = []
    for kind in range(2):
        pieces.append(pick(real_rows, kind, 0) + pick(imag_rows, kind, 1))
        pieces.append(pick(real_rows, kind, 1) - pick(imag_rows, kind, 0))
    part[...] = jnp.concatenate(pieces, axis=0)
    share = out_ref.shape[0]

    def block_of(index):
        return pl.ds(pl.multiple_of(index * share, share), share)

    for peer in others:
        copies.append(
            send_to(
                "pw", peer, part.at[block_of(peer)], parts.at[me], send_p.at[peer], recv_p.at[me]
            )
        )
    parts[me] = part[block_of(me), :]
    for peer in others:
        arrived("pw", peer, parts.at[peer], send_p.at[peer], recv_p.at[peer])
    total = parts[0]
    for d in range(1, parts.shape[0]):
        total = total + parts[d]
    out_ref[...] = total
    for copy in copies:
        copy.wait_send()


def last_part(slot, panel, columns, x, table, margin, slab, sizes, width, mates):
    devices = x.shape[0]
    cols = columns.shape[1]
    count, _, n = panel.shape
    steps = n // BLOCK
    size = 2 * count
    rows = slab.shape[0]
    groups = 3 if steps % 6 == 0 else 1
    share = 2 * mates * size // devices
    whole = pl.BlockSpec(memory_space=pltpu.VMEM)
    anywhere = pl.BlockSpec(memory_space=pl.ANY)
    dma = pltpu.SemaphoreType.DMA
    return pl.pallas_call(
        functools.partial(last_kernel, sizes, width, groups),
        in_specs=[whole] * 6 + [anywhere],
        out_specs=whole,
        out_shape=jax.ShapeDtypeStruct((share, rows), F32),
        scratch_shapes=[
            pltpu.VMEM(x.shape, BF16),
            pltpu.VMEM((count * width + 16, cols), BF16),
            pltpu.VMEM((steps, cols, BLOCK), BF16),
            pltpu.VMEM((1, n), F32),
            pltpu.VMEM((mates, 2, steps, 16, BLOCK * count // 16), BF16),
            pltpu.VMEM(slab.shape, BF16),
            pltpu.VMEM((2, mates * count * BLOCK // 128 // 128, rows * BLOCK // 64, 128), F32),
            pltpu.VMEM((2 * mates * size, rows), F32),
            pltpu.VMEM((devices, share, rows), F32),
            dma,
            dma((devices, 2)),
            dma((devices, 2)),
            dma((mates, 2, groups)),
            dma((mates, 2, groups)),
            dma((devices,)),
            dma((devices,)),
        ],
        compiler_params=pltpu.CompilerParams(
            vmem_limit_bytes=LIMIT, collective_id=2, has_side_effects=True
        ),
        name="last_part",
    )(slot, panel, columns, x, table, margin, slab)


def per_device(slab, panel, potential, pw_slot, columns):
    devices = lax.axis_size("pw")
    mates = lax.axis_size("band")
    planes, n_one, n_two = potential.shape
    length = planes * devices
    cols = columns.shape[0]
    count = panel.shape[0]
    n = panel.shape[2]

    square = disk_square(n_one, n_two, cols * devices)
    wide = odd_tiles(window(math.isqrt(square), 8, max(n_one, n_two)))
    reach = math.isqrt(square + (-(-n // (2 * cols)) + 2) ** 2) + 1
    width = window(reach, 16, length)

    ztab = jnp.asarray(z_tables(count // 2, length, planes, width), BF16)
    cy, sy = cos_sin(np.arange(n_two), signed_of(wide), n_two)
    cx, sx = cos_sin(np.arange(n_one), signed_of(wide), n_one)
    tables = [
        np.concatenate([cx, sx], axis=1),
        np.block([[cy, sy], [-sy, cy]]),
        np.concatenate([cy.T, -sy.T], axis=1),
        np.concatenate([cx.T, -sx.T], axis=1),
    ]
    tables = [jnp.asarray(t, BF16) for t in tables]

    slot = pw_slot.reshape(1, n)
    owned = columns.reshape(1, cols)
    sizes = (n_one, n_two, length)
    slab = slab.reshape(slab.shape[0], 2, n // 128, 128)
    slab = slab.transpose(0, 2, 1, 3).reshape(slab.shape[0], n // 64, 128)
    there, pos, margin = first_part(
        slot, panel, owned, ztab, slab, sizes, wide, width, devices, mates
    )
    worked = plane_part(
        pos.reshape(devices * cols), there, tables, potential.reshape(planes * n_one, n_two), wide, n_one, n_two
    )
    out = last_part(
        slot, panel, owned, worked, ztab, margin, slab, sizes, width, mates
    )
    return out.T


def solution(mesh):
    in_specs = (P("band", None, "pw"), P("band", None, "pw"), P("pw", None, None), P("pw"), P("pw"))
    out_specs = P("band", "pw")
    return jax.shard_map(
        per_device, mesh=mesh, in_specs=in_specs, out_specs=out_specs, check_vma=False
    )
```
